256 devices in a mesh: dom: 64 (over x_lo, z, y), edge: 4 (over x_hi, core).
Axes of the slice: x: 4 (x_hi: 2, x_lo: 2; x = x_hi * 2 + x_lo), y: 4, z: 8, core: 2. Of those that a mesh axis runs over, the one named last changes fastest.
Arguments:
- entity_emb: float32 [131072, 400], P('dom'), may hold values from -3 to 3
- entity_state: float32 [131072], P('dom'), may hold values from 4 to 1000
- relation_emb: float32 [7424, 400], P(('dom', 'edge')), may hold values from -1.5 to 1.5
- relation_state: float32 [7424], P(('dom', 'edge')), may hold values from 4 to 1000
- head_rows: int32 [2, 131072], P(None, ('dom', 'edge')), may hold values from 0 to 2047
- tail_rows: int32 [2, 131072], P(None, ('dom', 'edge')), may hold values from 0 to 2047
- relation_ids: int32 [2, 131072], P(None, ('dom', 'edge')), may hold values from 0 to 7423
- negative_rows: int32 [2, 256, 256], P(None, ('dom', 'edge')), may hold values from 0 to 2047
Outputs:
- new_entity_emb: float32 [131072, 400], P('dom')
- new_entity_state: float32 [131072], P('dom')
- new_relation_emb: float32 [7424, 400], P(('dom', 'edge'))
- new_relation_state: float32 [7424], P(('dom', 'edge'))
The draws below stay inside these ranges and needn't reach their ends.
All inputs are finite; a program needn't handle non-finite values.
Results may differ from the reference program's by a relative error of at most 0.0063.
Values may be sent and summed in bfloat16 or wider, within the bound.
A program may use at most 128 MiB of HBM per device.

```python
import math
import jax
import jax.numpy as jnp
import numpy as np
from jax import lax

D = 400
REL = 7424
NEG = 256
SPAN = 512
ROWS = 2048
EDGE_DEV = 512
ENTITIES = 131072
EDGES = 131072
SPANS = 256
N_DOM = 64
N_EDGE = 4


def plant(entries, stream_key, low, largest):
    index_at = [jax.random.randint(jax.random.fold_in(stream_key, axis), (), 0, length) for axis, length in enumerate(entries.shape)]
    widest = entries.shape.index(max(entries.shape))
    beside = index_at[:widest] + [(index_at[widest] + 1) % entries.shape[widest]] + index_at[widest + 1:]
    return entries.at[tuple(index_at)].set(low).at[tuple(beside)].set(largest)


def shard_levels(rng, shape, pieces, smallest, high):
    def one(axis_at, blocks):
        steps = jax.random.uniform(jax.random.fold_in(jax.random.fold_in(rng, 6), axis_at), (blocks,), jnp.float32, smallest / len(pieces), high / len(pieces))
        return jnp.repeat(jnp.exp(steps), shape[axis_at] // blocks).reshape((-1,) + (1,) * (len(shape) - axis_at - 1))

    level = one(*pieces[0])
    for cut in pieces[1:]:
        level = level * one(*cut)
    return level


def rank_table(number_of, slope):
    loads = [(1 << 20) // math.isqrt(grade ** slope) + 1 for grade in range(1, number_of + 1)]
    scale = 1 + sum(loads) // (1 << 30)
    return np.cumsum(np.array([max(1, weight // scale) for weight in loads]))


def ranked_ids(stream_key, shape, amount, skew):
    grid = rank_table(amount, skew)
    ticket = jax.random.randint(jax.random.fold_in(stream_key, 1), shape, 0, int(grid[amount - 1]))
    standing = jnp.searchsorted(jnp.asarray(grid, jnp.int32), ticket, side="right")
    return jax.random.permutation(jax.random.fold_in(stream_key, 2), amount)[standing].astype(jnp.int32)


def noise(stream_key, dims, width, most, split=(), kind=jnp.bfloat16):
    level = shard_levels(stream_key, dims, split, -0.22, 0.18) if split else 1.0
    array = jax.random.normal(stream_key, dims, jnp.float32) * width * level
    return jnp.minimum(jnp.maximum(array, -most), most).astype(kind)


def setup_inputs(seed: int = 0) -> dict:
    streams_of = jax.random.split(jax.random.key(seed), 9)
    return {
        "entity_emb": noise(streams_of[0], (ENTITIES, D), 0.5, 3.0, ((0, 64),), jnp.float32),
        "entity_state": jnp.clip(jnp.exp(math.log(1000.0) - 5.521461 * jax.random.uniform(streams_of[1], (ENTITIES,), jnp.float32) ** shard_levels(streams_of[1], (ENTITIES,), ((0, 64),), -0.2, 0.2)), 4.0, 1000.0),
        "relation_emb": noise(streams_of[2], (REL, D), 0.25, 1.5, ((0, 256),), jnp.float32),
        "relation_state": jnp.clip(jnp.exp(math.log(1000.0) - 5.521461 * jax.random.uniform(streams_of[3], (REL,), jnp.float32) ** shard_levels(streams_of[3], (REL,), ((0, 256),), -0.2, 0.2)), 4.0, 1000.0),
        "head_rows": plant(jax.random.randint(streams_of[4], (2, EDGES), 0, ROWS), jax.random.fold_in(streams_of[4], 1), 0, ROWS - 1).astype(jnp.int32),
        "tail_rows": plant(ranked_ids(streams_of[5], (2, EDGES), ROWS, 2), jax.random.fold_in(streams_of[5], 3), 0, ROWS - 1).astype(jnp.int32),
        "relation_ids": plant(jax.random.randint(streams_of[6], (2, EDGES), 0, REL), jax.random.fold_in(streams_of[6], 1), 0, REL - 1).astype(jnp.int32),
        "negative_rows": plant(jax.random.randint(streams_of[7], (2, SPANS, NEG), 0, ROWS), jax.random.fold_in(streams_of[7], 1), 0, ROWS - 1).astype(jnp.int32),
    }


LEARN_RATE = 0.5

def complex_times(left_side, right_side):
    middle = left_side.shape[-1] // 2
    left_real, left_imag = (left_side[..., :middle], left_side[..., middle:])
    right_real, right_imag = (right_side[..., :middle], right_side[..., middle:])
    return jnp.concatenate([left_real * right_real - left_imag * right_imag, left_real * right_imag + left_imag * right_real], axis=-1)

def complex_back(upstream, head_vec, rel_vec):
    middle = upstream.shape[-1] // 2
    up_real, up_imag = (upstream[..., :middle], upstream[..., middle:])
    head_real, head_imag = (head_vec[..., :middle], head_vec[..., middle:])
    rel_real, rel_imag = (rel_vec[..., :middle], rel_vec[..., middle:])
    head_grad = jnp.concatenate([up_real * rel_real + up_imag * rel_imag, up_imag * rel_real - up_real * rel_imag], axis=-1)
    rel_grad = jnp.concatenate([up_real * head_real + up_imag * head_imag, up_imag * head_real - up_real * head_imag], axis=-1)
    return (head_grad, rel_grad)

def bucket_terms(own_rows, partner_rows, relation_table, head_ids, tail_ids, relation_index, negatives):
    part_rows, features = own_rows.shape
    head_vec = own_rows[head_ids].astype(jnp.float32)
    tail_vec = partner_rows[tail_ids].astype(jnp.float32)
    rel_vec = relation_table[relation_index].astype(jnp.float32)
    queries = complex_times(head_vec, rel_vec)
    queries_low = queries.astype(jnp.bfloat16)
    positive = lax.optimization_barrier(jnp.sum(queries * tail_vec, axis=-1))
    blocks = negatives.shape[0]
    sampled_entities = partner_rows[negatives].astype(jnp.float32)
    grouped_rows = queries_low.astype(jnp.float32).reshape(blocks, -1, features)
    triple_scores = jnp.einsum('ymt,yst->yms', grouped_rows, sampled_entities, precision=lax.Precision.HIGHEST)
    pos_slope = -jax.nn.sigmoid(-positive)
    negative_gradient = jax.nn.sigmoid(triple_scores).astype(jnp.bfloat16).astype(jnp.float32)
    gathered_rows = jnp.einsum('zsm,zmi->zsi', negative_gradient, sampled_entities, precision=lax.Precision.HIGHEST)
    query_grad = pos_slope[:, None] * tail_vec + gathered_rows.reshape(-1, features)
    negative_sample_gradient = jnp.einsum('tyo,tyv->tov', negative_gradient, grouped_rows, precision=lax.Precision.HIGHEST)
    head_grad, rel_grad = complex_back(query_grad, head_vec, rel_vec)
    own_grad = jnp.zeros((part_rows, features), jnp.float32).at[head_ids].add(head_grad)
    partner_grad = jnp.zeros((part_rows, features), jnp.float32).at[tail_ids].add(pos_slope[:, None] * queries)
    partner_grad = partner_grad.at[negatives.reshape(-1)].add(negative_sample_gradient.reshape(-1, features))
    return (own_grad, partner_grad, rel_grad)

def adagrad(weights, history, gradient):
    new_history = history + lax.optimization_barrier(jnp.mean(gradient * gradient, axis=-1))
    return (weights - LEARN_RATE * gradient / jnp.sqrt(new_history)[:, None], new_history)

def reference(entity_emb, entity_state, relation_emb, relation_state, head_rows, tail_rows, relation_ids, negative_rows):
    low_all = entity_emb.astype(jnp.bfloat16).reshape(N_DOM, ROWS, D)
    relation_low = relation_emb.astype(jnp.bfloat16)
    head_all = head_rows.reshape(2, N_DOM, N_EDGE, EDGE_DEV)
    tail_all = tail_rows.reshape(2, N_DOM, N_EDGE, EDGE_DEV)
    rel_all = relation_ids.reshape(2, N_DOM, N_EDGE, EDGE_DEV)
    neg_all = negative_rows.reshape(2, N_DOM, N_EDGE, EDGE_DEV // SPAN, NEG)
    per_slot = jax.vmap(bucket_terms, in_axes=(None, None, None, 0, 0, 0, 0))

    def partition_step(running, index):
        entity_grad, relation_grad = running
        upper_index = (index + 1) % N_DOM
        lower_index = (index + N_DOM - 1) % N_DOM
        for entity_bucket, partner in ((0, upper_index), (1, lower_index)):
            own_grad, partner_grad, rel_grad = per_slot(low_all[index], low_all[partner], relation_low, head_all[entity_bucket, index], tail_all[entity_bucket, index], rel_all[entity_bucket, index], neg_all[entity_bucket, index])
            rounded = lax.optimization_barrier(partner_grad.astype(jnp.bfloat16)).astype(jnp.float32)
            entity_grad = entity_grad.at[index].add(lax.optimization_barrier(jnp.sum(own_grad, axis=0)))
            entity_grad = entity_grad.at[partner].add(lax.optimization_barrier(jnp.sum(rounded, axis=0)))
            relation_grad = relation_grad.at[rel_all[entity_bucket, index].reshape(-1)].add(rel_grad.reshape(-1, D))
        return ((entity_grad, relation_grad), None)
    start_state = (jnp.zeros((N_DOM, ROWS, D), jnp.float32), jnp.zeros((REL, D), jnp.float32))
    (entity_grad, relation_grad), _ = lax.scan(partition_step, start_state, jnp.arange(N_DOM, dtype=jnp.int32))
    new_entity_emb, new_entity_state = adagrad(entity_emb, entity_state, entity_grad.reshape(ENTITIES, D))
    new_relation_emb, new_relation_state = adagrad(relation_emb, relation_state, relation_grad)
    return (new_entity_emb, new_entity_state, new_relation_emb, new_relation_state)
```

```python
import jax
import jax.numpy as jnp
from jax import lax
from jax.experimental import pallas as pl
from jax.experimental.pallas import tpu as pltpu
from jax.sharding import PartitionSpec as P

LEARN_RATE = 0.5
D = 400
HALF = 200
ROWS = 2048
EDGES = 512
NEG = 256
OWN_REL = 29
SLOT = 32
CUT = 208
Z = 8
BLOCKS = 32
MIB = 1 << 20
MESH = pl.DeviceIdType.MESH
BF = jnp.bfloat16
F32 = jnp.float32

GATHER_ORDER = (0, -1, 1, -2, 2, -3, 3, 4)
SCATTER_ORDER = (4, 3, -3, 2, -2, 1, -1, 0)


class Place:
    def __init__(self):
        self.d = lax.axis_index("dom")
        self.e = lax.axis_index("edge")
        self.y = lax.rem(self.d, 4)
        self.z = lax.rem(self.d // 4, Z)
        self.xl = self.d // 32
        self.xh = self.e // 2
        self.c = lax.rem(self.e, 2)
        x = self.xh * 2 + self.xl
        other = lax.rem(self.d + 32, 64)
        self.x_up = (other, (lax.rem(x + 1, 4) // 2) * 2 + self.c)
        self.x_down = (other, (lax.rem(x + 3, 4) // 2) * 2 + self.c)
        self.z_up = (self.xl * 32 + lax.rem(self.z + 1, Z) * 4 + self.y, self.e)
        self.z_down = (self.xl * 32 + lax.rem(self.z + 7, Z) * 4 + self.y, self.e)
        self.next = (lax.rem(self.d + 1, 64), self.e)
        self.prev = (lax.rem(self.d + 63, 64), self.e)
        self.sibling = (self.d, self.xh * 2 + 1 - self.c)
        self.far = (self.d, (1 - self.xh) * 2 + self.c)

    def group(self, y, e):
        return (self.d - self.y + y, e)

    def block(self, xl, offset, half):
        return (xl * Z + lax.rem(self.z + offset + Z, Z)) * 2 + half


def greet(at):
    barrier = pltpu.get_barrier_semaphore()
    where = at.y * 4 + at.e
    for k in range(1, 16):
        peer = lax.rem(where + k, 16)
        pl.semaphore_signal(
            barrier, inc=1, device_id=at.group(peer // 4, lax.rem(peer, 4)), device_id_type=MESH
        )
    for peer in (at.x_up, at.x_down, at.z_up, at.z_down, at.next, at.prev):
        pl.semaphore_signal(barrier, inc=1, device_id=peer, device_id_type=MESH)
    pl.semaphore_wait(barrier, 21)


def send(src, dst, send_sem, recv_sem, peer):
    pltpu.make_async_remote_copy(
        src_ref=src,
        dst_ref=dst,
        send_sem=send_sem,
        recv_sem=recv_sem,
        device_id=peer,
        device_id_type=MESH,
    ).start()


def settle(ref, sem):
    pltpu.make_async_copy(ref, ref, sem).wait()


NP = 2
PW = ROWS // 2 // NP


def gather_kernel(
    shard, own, table, upper, lower, gath, blk,
    a_send, a_recv, z_send, z_recv, x_send, x_recv, s_send, s_recv, p_send, p_recv, q_send, q_recv, own_sem,
):
    at = Place()
    greet(at)

    slot = lax.rem(at.y, 2) * 4 + at.e
    row = pl.multiple_of(slot * SLOT, SLOT)
    here = at.c == at.y // 2
    mine = gath.at[pl.ds(row, SLOT), :]
    for k in range(8):
        y, xh = lax.rem(at.y + k // 2, 4), lax.rem(at.xh + k % 2, 2)
        peer = at.group(y, xh * 2 + at.y // 2)
        if k == 0:
            @pl.when(here)
            def _():
                pltpu.make_async_copy(shard, mine, a_recv.at[slot]).start()

            @pl.when(jnp.logical_not(here))
            def _():
                send(shard, mine, a_send.at[0], a_recv.at[slot], peer)
        else:
            send(shard, mine, a_send.at[k], a_recv.at[slot], peer)

    for n in range(NP):
        cols = pl.ds(pl.multiple_of(at.c * (ROWS // 2) + n * PW, PW), PW)
        send(own.at[:, cols], upper.at[:, cols], p_send.at[0, n], p_recv.at[0, n], at.prev)
        send(own.at[:, cols], lower.at[:, cols], p_send.at[1, n], p_recv.at[1, n], at.next)

    for k in range(8):
        settle(gath.at[pl.ds(k * SLOT, SLOT), :], a_recv.at[k])
    blk[...] = gath[...].astype(F32).T[:D].astype(BF)
    first = at.block(at.xl, 0, at.c)
    keep = pltpu.make_async_copy(blk, table.at[first], own_sem)
    keep.start()

    top, low = pl.ds(0, CUT), pl.ds(CUT, D - CUT)

    def index(j, xl=None):
        return at.block(at.xl if xl is None else xl, GATHER_ORDER[j], at.c)

    def whole(j):
        return blk if j == 0 else table.at[index(j)]

    def along_x(j, part):
        rows, peer = ((top, at.x_up), (low, at.x_down))[part]
        src = blk.at[rows, :] if j == 0 else table.at[index(j), rows, :]
        send(src, table.at[index(j), rows, :], x_send.at[part, j], x_recv.at[part, j], peer)

    def to_sibling(j, xl=None):
        n = index(j, xl)
        q = j if xl is None else 8 + j
        src = blk if q == 0 else table.at[n]
        send(src, table.at[n], s_send.at[q], s_recv.at[q], at.sibling)

    def along_z(way, step):
        j = (0, 2 * step - 1 + way)[step > 0]
        peer = (at.z_up, at.z_down)[way]
        if step < 3:
            send(whole(j), table.at[index(j)], z_send.at[way, step], z_recv.at[way, step], peer)
        else:
            rows = (top, low)[way]
            ref = table.at[index(j), rows, :]
            send(ref, ref, z_send.at[way, step], z_recv.at[way, step], peer)

    def from_x(j):
        n = index(j, 1 - at.xl)
        settle(table.at[n, top, :], x_recv.at[0, j])
        settle(table.at[n, low, :], x_recv.at[1, j])
        to_sibling(j, 1 - at.xl)

    along_z(0, 0)
    along_z(1, 0)
    along_x(0, 0)
    along_x(0, 1)
    to_sibling(0)
    for step in range(3):
        for way in range(2):
            j = 2 * step + 1 + way
            settle(table.at[index(j)], z_recv.at[way, step])
            along_z(way, step + 1)
            along_x(j, 0)
            along_x(j, 1)
            to_sibling(j)
        if step == 0:
            from_x(0)
        else:
            from_x(2 * step - 1)
            from_x(2 * step)
    settle(table.at[index(7), top, :], z_recv.at[0, 3])
    along_x(7, 0)
    settle(table.at[index(7), low, :], z_recv.at[1, 3])
    along_x(7, 1)
    to_sibling(7)
    from_x(5)
    from_x(6)
    for n in range(NP):
        cols = pl.ds(pl.multiple_of(at.c * (ROWS // 2) + n * PW, PW), PW)
        for way, ref in enumerate((upper, lower)):
            part = ref.at[:, cols]
            settle(part, p_recv.at[way, n])
            send(part, part, q_send.at[way, n], q_recv.at[way, n], at.sibling)
    from_x(7)

    for j in range(8):
        settle(table.at[at.block(at.xl, GATHER_ORDER[j], 1 - at.c)], s_recv.at[j])
        settle(table.at[at.block(1 - at.xl, GATHER_ORDER[j], 1 - at.c)], s_recv.at[8 + j])
    for n in range(NP):
        cols = pl.ds(pl.multiple_of((1 - at.c) * (ROWS // 2) + n * PW, PW), PW)
        settle(upper.at[:, cols], q_recv.at[0, n])
        settle(lower.at[:, cols], q_recv.at[1, n])
    keep.wait()

    @pl.when(jnp.logical_not(here))
    def _():
        settle(shard, a_send.at[0])

    for k in range(1, 8):
        settle(shard, a_send.at[k])
    for way in range(2):
        for n in range(NP):
            settle(upper.at[:, pl.ds(0, PW)], p_send.at[way, n])
            settle(upper.at[:, pl.ds(0, PW)], q_send.at[way, n])
        for step in range(3):
            settle(blk, z_send.at[way, step])
        settle(blk.at[(top, low)[way], :], z_send.at[way, 3])
        for j in range(8):
            settle(blk.at[(top, low)[way], :], x_send.at[way, j])
    for q in range(16):
        settle(blk, s_send.at[q])


def gather_all(shard, own):
    dma = pltpu.SemaphoreType.DMA
    part = jax.ShapeDtypeStruct((D, ROWS), BF)
    anywhere = pl.BlockSpec(memory_space=pl.ANY)
    return pl.pallas_call(
        gather_kernel,
        out_shape=(jax.ShapeDtypeStruct((BLOCKS, D, 256), BF), part, part),
        in_specs=[pl.BlockSpec(memory_space=pltpu.VMEM), anywhere],
        out_specs=(anywhere, anywhere, anywhere),
        scratch_shapes=[
            pltpu.VMEM((256, 512), BF),
            pltpu.VMEM((D, 256), BF),
            dma((8,)), dma((8,)),
            dma((2, 4)), dma((2, 4)),
            dma((2, 8)), dma((2, 8)),
            dma((16,)), dma((16,)),
            dma((2, NP)), dma((2, NP)),
            dma((2, NP)), dma((2, NP)),
            dma,
        ],
        compiler_params=pltpu.CompilerParams(
            collective_id=0, has_side_effects=True, vmem_limit_bytes=16 * MIB
        ),
        name="gather_all",
    )(shard, own)


def onehot(ids, base, rows):
    at = lax.broadcasted_iota(jnp.int32, (rows, ids.shape[1]), 0) + base
    return jnp.where(at == ids, 1.0, 0.0).astype(BF)


def dot(a, b, over=((1,), (0,))):
    return lax.dot_general(a, b, (over, ((), ())), preferred_element_type=F32)


ACROSS = ((1,), (1,))


def compute_kernel(
    own, upper, lower, table, heads, tails, negs, rels,
    own_out, upper_out, lower_out, table_out,
    head_vec, part_vec, rel_vec, head_grad, part_grad, rel_grad,
):
    def fetch(source, ids, out, cols):
        out[:, cols] = dot(source[:, :1024], onehot(ids, 0, 1024)) + dot(
            source[:, 1024:], onehot(ids, 1024, 1024)
        )

    for b, source in enumerate((upper, lower)):
        fetch(own, heads[b:b + 1, :], head_vec, pl.ds(b * EDGES, EDGES))
        fetch(source, tails[b:b + 1, :], part_vec, pl.ds(b * 768, EDGES))
        fetch(source, negs[b:b + 1, :], part_vec, pl.ds(b * 768 + EDGES, NEG))

    rel_vec[...] = jnp.zeros_like(rel_vec)

    @pl.loop(0, BLOCKS // 4)
    def _(k):
        for b in range(2):
            ids = rels[b:b + 1, :]
            total = None
            for i in range(4):
                term = dot(table[k * 4 + i], onehot(ids, (k * 4 + i) * 256, 256))
                total = term if total is None else total + term
            rel_vec[:, b * EDGES:(b + 1) * EDGES] += total

    for b in range(2):
        span = slice(b * EDGES, (b + 1) * EDGES)
        h_re, h_im = head_vec[:HALF, span], head_vec[HALF:, span]
        r_re, r_im = rel_vec[:HALF, span], rel_vec[HALF:, span]
        q = jnp.concatenate([h_re * r_re - h_im * r_im, h_re * r_im + h_im * r_re], axis=0)
        q_low = q.astype(BF)
        tail = part_vec[:, b * 768:b * 768 + EDGES]
        cand = part_vec[:, b * 768 + EDGES:(b + 1) * 768].astype(BF)
        positive = jnp.sum(q * tail, axis=0, keepdims=True)
        slope = -jax.nn.sigmoid(-positive)
        scores = dot(cand, q_low, ((0,), (0,)))
        neg_slope = jax.nn.sigmoid(scores).astype(BF)
        u = slope * tail + dot(cand, neg_slope)
        part_grad[b, :, :EDGES] = (slope * q).astype(BF)
        part_grad[b, :, EDGES:] = dot(q_low, neg_slope, ACROSS).astype(BF)
        u_re, u_im = u[:HALF], u[HALF:]
        head_grad[:, span] = jnp.concatenate(
            [u_re * r_re + u_im * r_im, u_im * r_re - u_re * r_im], axis=0
        ).astype(BF)
        rel_grad[:, span] = jnp.concatenate(
            [u_re * h_re + u_im * h_im, u_im * h_re - u_re * h_im], axis=0
        ).astype(BF)

    @pl.loop(0, BLOCKS)
    def _(k):
        table_out[k] = (
            dot(rel_grad[:, :EDGES], onehot(rels[0:1, :], k * 256, 256), ACROSS)
            + dot(rel_grad[:, EDGES:], onehot(rels[1:2, :], k * 256, 256), ACROSS)
        ).astype(BF)

    @pl.loop(0, ROWS // 256)
    def _(k):
        cols = pl.ds(pl.multiple_of(k * 256, 256), 256)
        own_out[:, cols] = (
            dot(head_grad[:, :EDGES], onehot(heads[0:1, :], k * 256, 256), ACROSS)
            + dot(head_grad[:, EDGES:], onehot(heads[1:2, :], k * 256, 256), ACROSS)
        ).astype(BF)
        for b, out in enumerate((upper_out, lower_out)):
            out[:, cols] = (
                dot(part_grad[b, :, :EDGES], onehot(tails[b:b + 1, :], k * 256, 256), ACROSS)
                + dot(part_grad[b, :, EDGES:], onehot(negs[b:b + 1, :], k * 256, 256), ACROSS)
            ).astype(BF)


def compute(own, upper, lower, table, heads, tails, negs, rels):
    part = jax.ShapeDtypeStruct((D, ROWS), BF)
    vmem = pl.BlockSpec(memory_space=pltpu.VMEM)
    return pl.pallas_call(
        compute_kernel,
        out_shape=(part, part, part, jax.ShapeDtypeStruct((BLOCKS, D, 256), BF)),
        in_specs=[vmem] * 8,
        out_specs=(vmem,) * 4,
        scratch_shapes=[
            pltpu.VMEM((D, 2 * EDGES), F32),
            pltpu.VMEM((D, 1536), F32),
            pltpu.VMEM((D, 2 * EDGES), F32),
            pltpu.VMEM((D, 2 * EDGES), BF),
            pltpu.VMEM((2, D, 768), BF),
            pltpu.VMEM((D, 2 * EDGES), BF),
        ],
        compiler_params=pltpu.CompilerParams(vmem_limit_bytes=56 * MIB),
        name="compute",
    )(own, upper, lower, table, heads, tails, negs, rels)


NE = 4
EW = ROWS // 2 // NE


def scatter_kernel(
    grads, own, upper, lower, rel_out, ent_out,
    sib, xs, xbuf, zs, zbuf, esib, es, fr, ss, far, fin, parts,
    s_send, s_recv, x_send, x_recv, z_send, z_recv, e_send, e_recv, n_send, n_recv,
    f_send, f_recv, g_send, g_recv, c_send, c_recv,
):
    at = Place()
    greet(at)
    top, low = pl.ds(0, CUT), pl.ds(CUT, D - CUT)
    halves = (top, low)
    tables = (upper, lower, own)

    def index(q, half):
        xl = 1 - at.xl if q < 8 else at.xl
        return at.block(xl, SCATTER_ORDER[q % 8], half)

    def swap(q):
        send(grads.at[index(q, 1 - at.c)], sib.at[q], s_send.at[q], s_recv.at[q], at.sibling)

    def cols_of(half, k):
        return pl.ds(pl.multiple_of(half * (ROWS // 2) + k * EW, EW), EW)

    def swap_part(t, k):
        send(
            tables[t].at[:, cols_of(1 - at.c, k)], esib.at[t, k],
            e_send.at[t, k], e_recv.at[t, k], at.sibling,
        )

    for k in range(NE):
        swap_part(0, k)
        swap_part(1, k)
        swap(2 * k)
        swap(2 * k + 1)
    for k in range(NE):
        swap(8 + 2 * k)
        swap(9 + 2 * k)
        swap_part(2, k)

    def both(q):
        settle(sib.at[q], s_recv.at[q])
        return grads[index(q, at.c)].astype(F32) + sib[q].astype(F32)

    def part_sum(t, k):
        settle(esib.at[t, k], e_recv.at[t, k])
        return tables[t][:, cols_of(at.c, k)].astype(F32) + esib[t, k].astype(F32)

    for k in range(NE):
        for t, peer in ((0, at.next), (1, at.prev)):
            es[t, k] = part_sum(t, k).astype(BF)
            send(es.at[t, k], fr.at[t, k], n_send.at[t, k], n_recv.at[t, k], peer)
        for j in (2 * k, 2 * k + 1):
            xs[j] = both(j).astype(BF)
            for part, peer in ((0, at.x_up), (1, at.x_down)):
                send(
                    xs.at[j, halves[part], :], xbuf.at[j, halves[part], :],
                    x_send.at[part, j], x_recv.at[part, j], peer,
                )

    def along_x(j):
        total = both(8 + j)
        settle(xbuf.at[j, top, :], x_recv.at[0, j])
        settle(xbuf.at[j, low, :], x_recv.at[1, j])
        return total + xbuf[j].astype(F32)

    def z_step(step):
        if step == 0:
            zs[0] = along_x(0).astype(BF)
            for way, peer in ((0, at.z_up), (1, at.z_down)):
                send(
                    zs.at[0, halves[way], :], zbuf.at[way, 0, halves[way], :],
                    z_send.at[way, 0], z_recv.at[way, 0], peer,
                )
            return
        for way, peer in ((0, at.z_up), (1, at.z_down)):
            j = 2 * step - 1 + way
            total = along_x(j)
            if step == 1:
                settle(zbuf.at[way, 0, halves[way], :], z_recv.at[way, 0])
                zs[j] = total.astype(BF)
                start, size = ((0, CUT), (CUT, D - CUT))[way]
                zs[j, start:start + size, :] = (
                    total[start:start + size] + zbuf[way, 0, start:start + size, :].astype(F32)
                ).astype(BF)
            else:
                settle(zbuf.at[way, step - 1], z_recv.at[way, step - 1])
                zs[j] = (total + zbuf[way, step - 1].astype(F32)).astype(BF)
            send(zs.at[j], zbuf.at[way, step], z_send.at[way, step], z_recv.at[way, step], peer)

    def part_step(k):
        total = part_sum(2, k)
        settle(fr.at[0, k], n_recv.at[0, k])
        settle(fr.at[1, k], n_recv.at[1, k])
        ss[k] = (total + fr[0, k].astype(F32) + fr[1, k].astype(F32)).astype(BF)
        send(ss.at[k], far.at[k], f_send.at[k], f_recv.at[k], at.far)

    def part_end(k):
        settle(far.at[k], f_recv.at[k])
        ent_out[:, cols_of(at.c, k)] = (ss[k].astype(F32) + far[k].astype(F32)).astype(BF)
        ref = ent_out.at[:, cols_of(at.c, k)]
        send(ref, ref, g_send.at[k], g_recv.at[k], at.sibling)

    z_step(0)
    part_step(0)
    z_step(1)
    part_step(1)
    z_step(2)
    part_step(2)
    z_step(3)
    part_step(3)
    part_end(0)
    part_end(1)

    total = along_x(7)
    for way in range(2):
        settle(zbuf.at[way, 3], z_recv.at[way, 3])
    total = total + zbuf[0, 3].astype(F32) + zbuf[1, 3].astype(F32)
    fin[...] = jnp.concatenate([total, jnp.zeros((512 - D, 256), F32)], axis=0).T
    source = at.y * 2 + at.xh
    for k in range(8):
        y, e = 2 * at.c + k // 4, k % 4
        here = jnp.logical_and(at.y == y, at.e == e)
        piece = fin.at[pl.ds(k * SLOT, SLOT), :]

        @pl.when(here)
        def _():
            pltpu.make_async_copy(piece, parts.at[source], c_recv.at[source]).start()

        @pl.when(jnp.logical_not(here))
        def _():
            send(piece, parts.at[source], c_send.at[k], c_recv.at[source], at.group(y, e))

    part_end(2)
    part_end(3)
    for k in range(8):
        settle(parts.at[k], c_recv.at[k])
    rel_out[...] = jnp.sum(parts[...], axis=0)

    for k in range(NE):
        settle(ent_out.at[:, cols_of(1 - at.c, k)], g_recv.at[k])
    for k in range(8):
        y, e = 2 * at.c + k // 4, k % 4

        @pl.when(jnp.logical_not(jnp.logical_and(at.y == y, at.e == e)))
        def _():
            settle(parts.at[k], c_send.at[k])

    for q in range(16):
        settle(sib.at[q], s_send.at[q])
    for k in range(NE):
        for t in range(3):
            settle(esib.at[t, k], e_send.at[t, k])
        for t in range(2):
            settle(es.at[t, k], n_send.at[t, k])
        settle(ss.at[k], f_send.at[k])
        settle(ss.at[k], g_send.at[k])
    for way in range(2):
        for j in range(8):
            settle(xs.at[j, halves[way], :], x_send.at[way, j])
        settle(zs.at[0, halves[way], :], z_send.at[way, 0])
        for step in range(1, 4):
            settle(zs.at[0], z_send.at[way, step])


def scatter_all(grads, own, upper, lower):
    dma = pltpu.SemaphoreType.DMA
    vmem = pl.BlockSpec(memory_space=pltpu.VMEM)
    block = (D, 256)
    return pl.pallas_call(
        scatter_kernel,
        out_shape=(
            jax.ShapeDtypeStruct((SLOT, 512), F32),
            jax.ShapeDtypeStruct((D, ROWS), BF),
        ),
        in_specs=[vmem] * 4,
        out_specs=(vmem, vmem),
        scratch_shapes=[
            pltpu.VMEM((16,) + block, BF),
            pltpu.VMEM((8,) + block, BF),
            pltpu.VMEM((8,) + block, BF),
            pltpu.VMEM((7,) + block, BF),
            pltpu.VMEM((2, 4) + block, BF),
            pltpu.VMEM((3, NE, D, EW), BF),
            pltpu.VMEM((2, NE, D, EW), BF),
            pltpu.VMEM((2, NE, D, EW), BF),
            pltpu.VMEM((NE, D, EW), BF),
            pltpu.VMEM((NE, D, EW), BF),
            pltpu.VMEM((256, 512), F32),
            pltpu.VMEM((8, SLOT, 512), F32),
            dma((16,)), dma((16,)),
            dma((2, 8)), dma((2, 8)),
            dma((2, 4)), dma((2, 4)),
            dma((3, NE)), dma((3, NE)),
            dma((2, NE)), dma((2, NE)),
            dma((NE,)), dma((NE,)),
            dma((NE,)), dma((NE,)),
            dma((8,)), dma((8,)),
        ],
        compiler_params=pltpu.CompilerParams(
            collective_id=1, has_side_effects=True, vmem_limit_bytes=56 * MIB
        ),
        name="scatter_all",
    )(grads, own, upper, lower)


def local(
    entity_emb,
    entity_state,
    relation_emb,
    relation_state,
    head_rows,
    tail_rows,
    relation_ids,
    negative_rows,
):
    entity = entity_emb.T
    own = entity.astype(BF)
    shard = jnp.pad(relation_emb.astype(BF), ((0, SLOT - OWN_REL), (0, 512 - D)))
    rels = relation_ids // OWN_REL * SLOT + relation_ids % OWN_REL
    table, upper, lower = gather_all(shard, own)
    own_part, upper_part, lower_part, grads = compute(
        own, upper, lower, table, head_rows, tail_rows, negative_rows[:, 0], rels
    )
    relation_grad, entity_grad = scatter_all(grads, own_part, upper_part, lower_part)

    entity_grad = entity_grad.astype(F32)
    new_entity_state = entity_state + jnp.mean(entity_grad * entity_grad, axis=0)
    new_entity = entity - LEARN_RATE * entity_grad / jnp.sqrt(new_entity_state)
    relation_grad = relation_grad[:OWN_REL, :D]
    new_relation_state = relation_state + jnp.mean(relation_grad * relation_grad, axis=-1)
    new_relation_emb = relation_emb - LEARN_RATE * relation_grad / jnp.sqrt(new_relation_state)[:, None]
    return (new_entity.T, new_entity_state, new_relation_emb, new_relation_state)


def solution(mesh):
    placed = (
        P("dom", None),
        P("dom"),
        P(("dom", "edge"), None),
        P(("dom", "edge")),
        P(None, ("dom", "edge")),
        P(None, ("dom", "edge")),
        P(None, ("dom", "edge")),
        P(None, ("dom", "edge"), None),
    )
    return jax.shard_map(
        local,
        mesh=mesh,
        in_specs=placed,
        out_specs=(P("dom", None), P("dom"), P(("dom", "edge"), None), P(("dom", "edge"))),
        check_vma=False,
    )
```

```python
import jax
import jax.numpy as jnp
from jax import lax
from jax.experimental import pallas as pl
from jax.experimental.pallas import tpu as pltpu
from jax.sharding import PartitionSpec as P

LEARN_RATE = 0.5
D = 400
HALF = 200
ROWS = 2048
EDGES = 512
NEG = 256
PICKS = EDGES + NEG
OWN_REL = 29
SLOT = 32
CUT = 208
Z = 8
BLOCKS = 32
MIB = 1 << 20
MESH = pl.DeviceIdType.MESH
BF = jnp.bfloat16
F32 = jnp.float32
ACROSS = ((1,), (1,))


class Place:
    def __init__(self):
        self.d = lax.axis_index("dom")
        self.e = lax.axis_index("edge")
        self.y = lax.rem(self.d, 4)
        self.z = lax.rem(self.d // 4, Z)
        self.xl = self.d // 32
        self.xh = self.e // 2
        self.c = lax.rem(self.e, 2)
        x = self.xh * 2 + self.xl
        other = lax.rem(self.d + 32, 64)
        self.x_up = (other, (lax.rem(x + 1, 4) // 2) * 2 + self.c)
        self.x_down = (other, (lax.rem(x + 3, 4) // 2) * 2 + self.c)
        self.z_up = self.along_z(0)
        self.z_down = self.along_z(1)
        self.next = (lax.rem(self.d + 1, 64), self.e)
        self.prev = (lax.rem(self.d + 63, 64), self.e)
        self.sibling = (self.d, self.xh * 2 + 1 - self.c)
        self.far = (self.d, (1 - self.xh) * 2 + self.c)

    def along_z(self, way):
        return (self.xl * 32 + lax.rem(self.z + 1 + 6 * way, Z) * 4 + self.y, self.e)

    def group(self, y, e):
        return (self.d - self.y + y, e)

    def block(self, xl, offset, half):
        return (xl * Z + lax.rem(self.z + offset + Z, Z)) * 2 + half

    def incoming(self, j, xl, half):
        return self.block(xl, jnp.where(j % 2 == 1, -((j + 1) // 2), j // 2), half)

    def outgoing(self, j, xl, half):
        away = 4 - (j + 1) // 2
        return self.block(xl, jnp.where(j % 2 == 1, away, -away), half)


def greet(at):
    barrier = pltpu.get_barrier_semaphore()
    where = at.y * 4 + at.e
    for k in range(1, 16):
        peer = lax.rem(where + k, 16)
        pl.semaphore_signal(
            barrier, inc=1, device_id=at.group(peer // 4, lax.rem(peer, 4)), device_id_type=MESH
        )
    for peer in (at.x_up, at.x_down, at.z_up, at.z_down, at.next, at.prev):
        pl.semaphore_signal(barrier, inc=1, device_id=peer, device_id_type=MESH)
    pl.semaphore_wait(barrier, 21)


def send(src, dst, send_sem, recv_sem, peer):
    pltpu.make_async_remote_copy(
        src_ref=src,
        dst_ref=dst,
        send_sem=send_sem,
        recv_sem=recv_sem,
        device_id=peer,
        device_id_type=MESH,
    ).start()


def settle(ref, sem):
    pltpu.make_async_copy(ref, ref, sem).wait()


def onehot(ids, base, rows):
    at = lax.broadcasted_iota(jnp.int32, (rows, ids.shape[1]), 0) + base
    return jnp.where(at == ids, 1.0, 0.0).astype(BF)


def dot(a, b, over=((1,), (0,))):
    return lax.dot_general(a, b, (over, ((), ())), preferred_element_type=F32)


def lanes(k):
    return pl.ds(pl.multiple_of(k * 256, 256), 256)


BLOCK = (D, 256)
DMA = pltpu.SemaphoreType.DMA
BUFFERS = (
    ("pad", (SLOT, 512), F32),
    ("shard", (SLOT, 512), BF),
    ("own", (D, ROWS), BF),
    ("rels", (2, EDGES), jnp.int32),
    ("ids_out", (2, 8, PICKS), jnp.int32),
    ("ids", (2, 8, PICKS), jnp.int32),
    ("gath", (256, 512), BF),
    ("table", (BLOCKS,) + BLOCK, BF),
    ("served", (2, 3) + BLOCK, BF),
    ("picked", (2, 3) + BLOCK, BF),
    ("head_vec", (D, 2 * EDGES), F32),
    ("rel_vec", (D, 2 * EDGES), F32),
    ("head_grad", (D, 2 * EDGES), BF),
    ("rel_grad", (D, 2 * EDGES), BF),
    ("pick_grad", (2, 3) + BLOCK, BF),
    ("pick_in", (2, 3) + BLOCK, BF),
    ("stage", (16,) + BLOCK, BF),
    ("sib", (16,) + BLOCK, BF),
    ("xs", (8,) + BLOCK, BF),
    ("xbuf", (8,) + BLOCK, BF),
    ("acc", BLOCK, F32),
    ("zs", (7,) + BLOCK, BF),
    ("zbuf", (2, 4) + BLOCK, BF),
    ("head_sum", (8,) + BLOCK, F32),
    ("ent_stage", (4,) + BLOCK, BF),
    ("ent_sib", (4,) + BLOCK, BF),
    ("ent_sum", (4,) + BLOCK, BF),
    ("ent_far", (4,) + BLOCK, BF),
    ("ent_end", (8,) + BLOCK, BF),
    ("fin", (256, 512), F32),
    ("parts", (8, SLOT, 512), F32),
)
SEMAPHORES = (
    ("a", (8,)), ("i", (2,)), ("p", (2, 3)), ("z", (2, 4)), ("x", (2, 8)), ("s", (16,)),
    ("n", (2, 3)), ("t", (16,)), ("w", (2, 8)), ("v", (2, 4)),
    ("es", (4,)), ("ef", (4,)), ("ee", (4,)), ("c", (8,)),
)


class Held:
    pass


def step_kernel(entity, relation, heads, tails, negs, relation_ids, rel_out, ent_out, *scratch):
    m = Held()
    names = [name for name, _, _ in BUFFERS]
    for name, _ in SEMAPHORES:
        names += [name + "_send", name + "_recv"]
    for name, ref in zip(names, scratch, strict=True):
        setattr(m, name, ref)
    at = Place()
    top, low = pl.ds(0, CUT), pl.ds(CUT, D - CUT)
    halves = (top, low)

    m.own[...] = entity[...].astype(BF)
    m.pad[...] = jnp.zeros_like(m.pad)
    m.pad[:OWN_REL, :D] = relation[...]
    m.shard[...] = m.pad[...].astype(BF)
    for b in range(2):
        m.ids_out[b, :, :EDGES] = jnp.broadcast_to(tails[b:b + 1, :], (8, EDGES))
        m.ids_out[b, :, EDGES:] = jnp.broadcast_to(negs[b], (8, NEG))
    ids = relation_ids[...]
    m.rels[...] = ids + (SLOT - OWN_REL) * ((ids * 36158) >> 20)
    greet(at)

    slot = lax.rem(at.y, 2) * 4 + at.e
    here = at.c == at.y // 2
    mine = m.gath.at[pl.ds(pl.multiple_of(slot * SLOT, SLOT), SLOT), :]
    for k in range(8):
        y, xh = lax.rem(at.y + k // 2, 4), lax.rem(at.xh + k % 2, 2)
        peer = at.group(y, xh * 2 + at.y // 2)
        if k == 0:
            @pl.when(here)
            def _():
                pltpu.make_async_copy(m.shard, mine, m.a_recv.at[slot]).start()

            @pl.when(jnp.logical_not(here))
            def _():
                send(m.shard, mine, m.a_send.at[0], m.a_recv.at[slot], peer)
        else:
            send(m.shard, mine, m.a_send.at[k], m.a_recv.at[slot], peer)
    for b, peer in enumerate((at.next, at.prev)):
        send(m.ids_out.at[b], m.ids.at[b], m.i_send.at[b], m.i_recv.at[b], peer)

    for k in range(8):
        settle(m.gath.at[pl.ds(k * SLOT, SLOT), :], m.a_recv.at[k])
    m.table[at.block(at.xl, 0, at.c)] = m.gath[...].astype(F32).T[:D].astype(BF)

    def along_z(j, way, step):
        ref = m.table.at[at.incoming(j, at.xl, at.c)]
        send(ref, ref, m.z_send.at[way, step], m.z_recv.at[way, step], at.along_z(way))

    def half_along_z(j, way):
        ref = m.table.at[at.incoming(j, at.xl, at.c), halves[way], :]
        send(ref, ref, m.z_send.at[way, 3], m.z_recv.at[way, 3], at.along_z(way))

    def along_x(j):
        for way, peer in ((0, at.x_up), (1, at.x_down)):
            ref = m.table.at[at.incoming(j, at.xl, at.c), halves[way], :]
            send(ref, ref, m.x_send.at[way, j], m.x_recv.at[way, j], peer)

    def to_sibling(j, xl, q):
        ref = m.table.at[at.incoming(j, xl, at.c)]
        send(ref, ref, m.s_send.at[q], m.s_recv.at[q], at.sibling)

    along_z(0, 0, 0)
    along_z(0, 1, 0)
    along_x(0)
    to_sibling(0, at.xl, 0)

    for b in range(2):
        settle(m.ids.at[b], m.i_recv.at[b])

    @pl.loop(0, 6)
    def _(t):
        b, n = t // 3, t % 3
        m.served[b, n] = dot(m.own[...], onehot(m.ids[b, 0:1, lanes(n)], 0, ROWS)).astype(BF)
        send(
            m.served.at[b, n], m.picked.at[b, n], m.p_send.at[b, n], m.p_recv.at[b, n],
            (lax.rem(at.d + 63 + 2 * b, 64), at.e),
        )

    m.rel_vec[...] = jnp.zeros_like(m.rel_vec)

    def head_rows(t):
        m.head_vec[:, lanes(t)] = dot(
            m.own[...], onehot(heads[pl.ds(t // 2, 1), lanes(t % 2)], 0, ROWS)
        )

    @pl.loop(1, 10)
    def _(j):
        way = (j + 1) % 2

        @pl.when(j <= 6)
        def _():
            settle(m.table.at[at.incoming(j, at.xl, at.c)], m.z_recv.at[way, (j - 1) // 2])

        @pl.when(j == 7)
        def _():
            for side in range(2):
                settle(m.table.at[at.incoming(j, at.xl, at.c), halves[side], :], m.z_recv.at[side, 3])

        @pl.when(j <= 4)
        def _():
            along_z(j, way, (j + 1) // 2)

        @pl.when(j == 5)
        def _():
            half_along_z(j, 0)

        @pl.when(j == 6)
        def _():
            half_along_z(j, 1)

        @pl.when(j <= 7)
        def _():
            along_x(j)
            to_sibling(j, at.xl, j)

        @pl.when(j <= 8)
        def _():
            for side in range(2):
                settle(
                    m.table.at[at.incoming(j - 1, 1 - at.xl, at.c), halves[side], :],
                    m.x_recv.at[side, j - 1],
                )
            to_sibling(j - 1, 1 - at.xl, 7 + j)

        @pl.when(j <= 4)
        def _():
            head_rows(j - 1)

        @pl.when(j >= 2)
        def _():
            k = j - 2
            for xl, q in ((at.xl, k), (1 - at.xl, 8 + k)):
                settle(m.table.at[at.incoming(k, xl, 1 - at.c)], m.s_recv.at[q])
            for b in range(2):
                total = None
                for xl in range(2):
                    for half in range(2):
                        n = at.incoming(k, xl, half)
                        term = dot(m.table[n], onehot(m.rels[b:b + 1, :], n * 256, 256))
                        total = term if total is None else total + term
                m.rel_vec[:, b * EDGES:(b + 1) * EDGES] += total

    for b in range(2):
        for n in range(3):
            settle(m.picked.at[b, n], m.p_recv.at[b, n])
        span = slice(b * EDGES, (b + 1) * EDGES)
        h_re, h_im = m.head_vec[:HALF, span], m.head_vec[HALF:, span]
        r_re, r_im = m.rel_vec[:HALF, span], m.rel_vec[HALF:, span]
        q = jnp.concatenate([h_re * r_re - h_im * r_im, h_re * r_im + h_im * r_re], axis=0)
        q_low = q.astype(BF)
        tail = jnp.concatenate([m.picked[b, 0], m.picked[b, 1]], axis=1).astype(F32)
        cand = m.picked[b, 2]
        positive = jnp.sum(q * tail, axis=0, keepdims=True)
        slope = -jax.nn.sigmoid(-positive)
        scores = dot(cand, q_low, ((0,), (0,)))
        neg_slope = jax.nn.sigmoid(scores).astype(BF)
        tail_grad = (slope * q).astype(BF)
        m.pick_grad[b, 0] = tail_grad[:, :256]
        m.pick_grad[b, 1] = tail_grad[:, 256:]
        m.pick_grad[b, 2] = dot(q_low, neg_slope, ACROSS).astype(BF)
        for n in range(3):
            send(
                m.pick_grad.at[b, n], m.pick_in.at[b, n], m.n_send.at[b, n], m.n_recv.at[b, n],
                (at.next, at.prev)[b],
            )
        u = slope * tail + dot(cand, neg_slope)
        u_re, u_im = u[:HALF], u[HALF:]
        m.rel_grad[:, span] = jnp.concatenate(
            [u_re * h_re + u_im * h_im, u_im * h_re - u_re * h_im], axis=0
        ).astype(BF)
        m.head_grad[:, span] = jnp.concatenate(
            [u_re * r_re + u_im * r_im, u_im * r_re - u_re * r_im], axis=0
        ).astype(BF)

    def rel_block(n):
        return dot(
            m.rel_grad[:, :EDGES], onehot(m.rels[0:1, :], n * 256, 256), ACROSS
        ) + dot(m.rel_grad[:, EDGES:], onehot(m.rels[1:2, :], n * 256, 256), ACROSS)

    def swap(j, xl, q):
        m.stage[q] = rel_block(at.outgoing(j, xl, 1 - at.c)).astype(BF)
        send(m.stage.at[q], m.sib.at[q], m.t_send.at[q], m.t_recv.at[q], at.sibling)

    @pl.loop(0, 9)
    def _(j):
        @pl.when(j < 8)
        def _():
            swap(j, 1 - at.xl, j)

        @pl.when(j > 0)
        def _():
            k = j - 1
            total = rel_block(at.outgoing(k, 1 - at.xl, at.c))
            settle(m.sib.at[k], m.t_recv.at[k])
            m.xs[k] = (total + m.sib[k].astype(F32)).astype(BF)
            for side, peer in ((0, at.x_up), (1, at.x_down)):
                send(
                    m.xs.at[k, halves[side], :], m.xbuf.at[k, halves[side], :],
                    m.w_send.at[side, k], m.w_recv.at[side, k], peer,
                )

    @pl.loop(0, 8)
    def _(j):
        swap(j, at.xl, 8 + j)

    def head_part(n):
        m.head_sum[n] = dot(
            m.head_grad[:, :EDGES], onehot(heads[0:1, :], n * 256, 256), ACROSS
        ) + dot(m.head_grad[:, EDGES:], onehot(heads[1:2, :], n * 256, 256), ACROSS)

    def entity_block(n):
        total = m.head_sum[n]
        for b in range(2):
            for i in range(3):
                ids = m.ids[b, 0:1, i * 256:(i + 1) * 256]
                total = total + dot(m.pick_in[b, i], onehot(ids, n * 256, 256), ACROSS)
        return total

    def entity_swap(k):
        m.ent_stage[k] = entity_block((1 - at.c) * 4 + k).astype(BF)
        send(m.ent_stage.at[k], m.ent_sib.at[k], m.es_send.at[k], m.es_recv.at[k], at.sibling)

    def entity_far(k):
        total = entity_block(at.c * 4 + k)
        settle(m.ent_sib.at[k], m.es_recv.at[k])
        m.ent_sum[k] = (total + m.ent_sib[k].astype(F32)).astype(BF)
        send(m.ent_sum.at[k], m.ent_far.at[k], m.ef_send.at[k], m.ef_recv.at[k], at.far)

    @pl.loop(0, 8)
    def _(j):
        total = rel_block(at.outgoing(j, at.xl, at.c))
        settle(m.sib.at[8 + j], m.t_recv.at[8 + j])
        for side in range(2):
            settle(m.xbuf.at[j, halves[side], :], m.w_recv.at[side, j])
        m.acc[...] = total + m.sib[8 + j].astype(F32) + m.xbuf[j].astype(F32)
        way, step = (j + 1) % 2, (j + 1) // 2

        for side in range(2):
            @pl.when(j == side + 1)
            def _():
                settle(m.zbuf.at[side, 0, halves[side], :], m.v_recv.at[side, 0])
                rows = (slice(0, CUT), slice(CUT, D))[side]
                m.acc[rows, :] += m.zbuf[side, 0, rows, :].astype(F32)

        @pl.when(jnp.logical_and(j >= 3, j <= 6))
        def _():
            settle(m.zbuf.at[way, step - 1], m.v_recv.at[way, step - 1])
            m.acc[...] += m.zbuf[way, step - 1].astype(F32)

        @pl.when(j == 0)
        def _():
            m.zs[0] = m.acc[...].astype(BF)
            for side in range(2):
                send(
                    m.zs.at[0, halves[side], :], m.zbuf.at[side, 0, halves[side], :],
                    m.v_send.at[side, 0], m.v_recv.at[side, 0], at.along_z(side),
                )

        @pl.when(jnp.logical_and(j >= 1, j <= 6))
        def _():
            m.zs[j] = m.acc[...].astype(BF)
            send(
                m.zs.at[j], m.zbuf.at[way, step], m.v_send.at[way, step], m.v_recv.at[way, step],
                at.along_z(way),
            )

        @pl.when(j < 4)
        def _():
            head_part(2 * j)
            head_part(2 * j + 1)

        @pl.when(j == 4)
        def _():
            for b in range(2):
                for n in range(3):
                    settle(m.pick_in.at[b, n], m.n_recv.at[b, n])

        @pl.when(jnp.logical_or(j == 4, j == 5))
        def _():
            @pl.loop(0, 2)
            def _(i):
                entity_swap(2 * (j - 4) + i)

        @pl.when(j >= 6)
        def _():
            @pl.loop(0, 2)
            def _(i):
                entity_far(2 * (j - 6) + i)

    for side in range(2):
        settle(m.zbuf.at[side, 3], m.v_recv.at[side, 3])
    total = m.acc[...] + m.zbuf[0, 3].astype(F32) + m.zbuf[1, 3].astype(F32)
    m.fin[...] = jnp.concatenate([total, jnp.zeros((512 - D, 256), F32)], axis=0).T
    source = at.y * 2 + at.xh
    for k in range(8):
        y, e = 2 * at.c + k // 4, k % 4
        mine_too = jnp.logical_and(at.y == y, at.e == e)
        piece = m.fin.at[pl.ds(k * SLOT, SLOT), :]

        @pl.when(mine_too)
        def _():
            pltpu.make_async_copy(piece, m.parts.at[source], m.c_recv.at[source]).start()

        @pl.when(jnp.logical_not(mine_too))
        def _():
            send(piece, m.parts.at[source], m.c_send.at[k], m.c_recv.at[source], at.group(y, e))

    @pl.loop(0, 4)
    def _(k):
        settle(m.ent_far.at[k], m.ef_recv.at[k])
        n = at.c * 4 + k
        m.ent_end[n] = (m.ent_sum[k].astype(F32) + m.ent_far[k].astype(F32)).astype(BF)
        send(m.ent_end.at[n], m.ent_end.at[n], m.ee_send.at[k], m.ee_recv.at[k], at.sibling)

    for k in range(8):
        settle(m.parts.at[k], m.c_recv.at[k])
    rel_out[...] = jnp.sum(m.parts[...], axis=0)
    for k in range(4):
        settle(m.ent_end.at[(1 - at.c) * 4 + k], m.ee_recv.at[k])
    for n in range(8):
        ent_out[:, n * 256:(n + 1) * 256] = m.ent_end[n]

    @pl.when(jnp.logical_not(here))
    def _():
        settle(m.shard, m.a_send.at[0])

    for k in range(1, 8):
        settle(m.shard, m.a_send.at[k])
    for k in range(8):
        y, e = 2 * at.c + k // 4, k % 4

        @pl.when(jnp.logical_not(jnp.logical_and(at.y == y, at.e == e)))
        def _():
            settle(m.parts.at[0], m.c_send.at[k])

    one = m.stage.at[0]
    for b in range(2):
        settle(m.ids_out.at[b], m.i_send.at[b])
        for n in range(3):
            settle(one, m.p_send.at[b, n])
            settle(one, m.n_send.at[b, n])
        half = m.stage.at[0, halves[b], :]
        for step in range(3):
            settle(one, m.z_send.at[b, step])
            settle(one, m.v_send.at[b, step + 1])
        settle(half, m.z_send.at[b, 3])
        settle(half, m.v_send.at[b, 0])
        for j in range(8):
            settle(half, m.x_send.at[b, j])
            settle(half, m.w_send.at[b, j])
    for q in range(16):
        settle(one, m.s_send.at[q])
        settle(one, m.t_send.at[q])
    for k in range(4):
        settle(one, m.es_send.at[k])
        settle(one, m.ef_send.at[k])
        settle(one, m.ee_send.at[k])


def whole_step(entity, relation, heads, tails, negs, relation_ids):
    vmem = pl.BlockSpec(memory_space=pltpu.VMEM)
    scratch = [pltpu.VMEM(shape, kind) for _, shape, kind in BUFFERS]
    for _, shape in SEMAPHORES:
        scratch += [DMA(shape), DMA(shape)]
    return pl.pallas_call(
        step_kernel,
        out_shape=(
            jax.ShapeDtypeStruct((SLOT, 512), F32),
            jax.ShapeDtypeStruct((D, ROWS), BF),
        ),
        in_specs=[vmem] * 6,
        out_specs=(vmem, vmem),
        scratch_shapes=scratch,
        compiler_params=pltpu.CompilerParams(
            collective_id=0, has_side_effects=True, vmem_limit_bytes=60 * MIB
        ),
        name="whole_step",
    )(entity, relation, heads, tails, negs, relation_ids)


def local(
    entity_emb,
    entity_state,
    relation_emb,
    relation_state,
    head_rows,
    tail_rows,
    relation_ids,
    negative_rows,
):
    entity = entity_emb.T
    relation_grad, entity_grad = whole_step(
        entity, relation_emb, head_rows, tail_rows, negative_rows, relation_ids
    )
    entity_grad = entity_grad.astype(F32)
    new_entity_state = entity_state + jnp.mean(entity_grad * entity_grad, axis=0)
    new_entity = entity - LEARN_RATE * entity_grad / jnp.sqrt(new_entity_state)
    relation_grad = relation_grad[:OWN_REL, :D]
    new_relation_state = relation_state + jnp.mean(relation_grad * relation_grad, axis=-1)
    new_relation_emb = relation_emb - LEARN_RATE * relation_grad / jnp.sqrt(new_relation_state)[:, None]
    return (new_entity.T, new_entity_state, new_relation_emb, new_relation_state)


def solution(mesh):
    placed = (
        P("dom", None),
        P("dom"),
        P(("dom", "edge"), None),
        P(("dom", "edge")),
        P(None, ("dom", "edge")),
        P(None, ("dom", "edge")),
        P(None, ("dom", "edge")),
        P(None, ("dom", "edge"), None),
    )
    return jax.shard_map(
        local,
        mesh=mesh,
        in_specs=placed,
        out_specs=(P("dom", None), P("dom"), P(("dom", "edge"), None), P(("dom", "edge"))),
        check_vma=False,
    )
```

```python
import jax
import jax.numpy as jnp
from jax import lax
from jax.experimental import pallas as pl
from jax.experimental.pallas import tpu as pltpu
from jax.sharding import PartitionSpec as P

LEARN_RATE = 0.5
D = 400
HALF = 200
ROWS = 2048
EDGES = 512
NEG = 256
PICKS = EDGES + NEG
OWN_REL = 29
SLOT = 32
CUT = 208
Z = 8
BLOCKS = 32
MIB = 1 << 20
MESH = pl.DeviceIdType.MESH
BF = jnp.bfloat16
F32 = jnp.float32
ACROSS = ((1,), (1,))


class Place:
    def __init__(self):
        self.d = lax.axis_index("dom")
        self.e = lax.axis_index("edge")
        self.y = lax.rem(self.d, 4)
        self.z = lax.rem(self.d // 4, Z)
        self.xl = self.d // 32
        self.even = jnp.logical_and(self.y > 0, self.y < 3)
        self.xh = self.e // 2
        self.c = lax.rem(self.e, 2)
        x = self.xh * 2 + self.xl
        other = lax.rem(self.d + 32, 64)
        self.x_up = (other, (lax.rem(x + 1, 4) // 2) * 2 + self.c)
        self.x_down = (other, (lax.rem(x + 3, 4) // 2) * 2 + self.c)
        self.z_up = self.along_z(0)
        self.z_down = self.along_z(1)
        self.next = (lax.rem(self.d + 1, 64), self.e)
        self.prev = (lax.rem(self.d + 63, 64), self.e)
        self.sibling = (self.d, self.xh * 2 + 1 - self.c)
        self.far = (self.d, (1 - self.xh) * 2 + self.c)

    def along_z(self, way):
        return (self.xl * 32 + lax.rem(self.z + 1 + 6 * way, Z) * 4 + self.y, self.e)

    def group(self, y, e):
        return (self.d - self.y + y, e)

    def block(self, xl, offset, half):
        return (xl * Z + lax.rem(self.z + offset + Z, Z)) * 2 + half

    def ring_step(self, j):
        return (jnp.where(self.even, 0x32211000, 0x43121000) >> (4 * jnp.minimum(j, 7))) & 15

    def ring_way(self, j):
        return (jnp.where(self.even, 0x54, jnp.where(self.y == 0, 0x24, 0xDA)) >> j) & 1

    def ring_sent(self, way, step, part):
        most = jnp.where(self.even, jnp.where(part == way, 4, 3), jnp.where(way == self.y // 3, 5, 2))
        return step < most

    def incoming(self, j, xl, half):
        away = self.ring_step(j) + 1
        away = jnp.where(self.ring_way(j) == 1, away, -away)
        return self.block(xl, jnp.where(j == 0, 0, away), half)

    def outgoing(self, j, xl, half):
        away = 4 - (j + 1) // 2
        return self.block(xl, jnp.where(j % 2 == 1, away, -away), half)


def greet(at):
    barrier = pltpu.get_barrier_semaphore()
    where = at.y * 4 + at.e
    for k in range(1, 16):
        peer = lax.rem(where + k, 16)
        pl.semaphore_signal(
            barrier, inc=1, device_id=at.group(peer // 4, lax.rem(peer, 4)), device_id_type=MESH
        )
    for peer in (at.x_up, at.x_down, at.z_up, at.z_down, at.next, at.prev):
        pl.semaphore_signal(barrier, inc=1, device_id=peer, device_id_type=MESH)
    return barrier


def send(src, dst, send_sem, recv_sem, peer):
    pltpu.make_async_remote_copy(
        src_ref=src,
        dst_ref=dst,
        send_sem=send_sem,
        recv_sem=recv_sem,
        device_id=peer,
        device_id_type=MESH,
    ).start()


def settle(ref, sem):
    pltpu.make_async_copy(ref, ref, sem).wait()


def onehot(ids, base, rows):
    at = lax.broadcasted_iota(jnp.int32, (rows, ids.shape[1]), 0) + base
    return jnp.where(at == ids, 1.0, 0.0).astype(BF)


def dot(a, b, over=((1,), (0,))):
    return lax.dot_general(a, b, (over, ((), ())), preferred_element_type=F32)


def lanes(k):
    return pl.ds(pl.multiple_of(k * 256, 256), 256)


BLOCK = (D, 256)
DMA = pltpu.SemaphoreType.DMA
BUFFERS = (
    ("entity", (D, ROWS), F32),
    ("pad", (SLOT, 512), F32),
    ("shard", (SLOT, 512), BF),
    ("own", (D, ROWS), BF),
    ("rels", (2, EDGES), jnp.int32),
    ("ids_out", (2, 8, PICKS), jnp.int32),
    ("ids", (2, 8, PICKS), jnp.int32),
    ("gath", (256, 512), BF),
    ("table", (BLOCKS,) + BLOCK, BF),
    ("served", (2, 3) + BLOCK, BF),
    ("picked", (2, 3) + BLOCK, BF),
    ("head_vec", (D, 2 * EDGES), F32),
    ("rel_vec", (D, 2 * EDGES), F32),
    ("head_grad", (D, 2 * EDGES), BF),
    ("rel_grad", (D, 2 * EDGES), BF),
    ("pick_grad", (2, 3) + BLOCK, BF),
    ("pick_in", (2, 3) + BLOCK, BF),
    ("stage", (16,) + BLOCK, BF),
    ("sib", (16,) + BLOCK, BF),
    ("xs", (8,) + BLOCK, BF),
    ("xbuf", (8,) + BLOCK, BF),
    ("acc", BLOCK, F32),
    ("zs", (7,) + BLOCK, BF),
    ("zbuf", (2, 4) + BLOCK, BF),
    ("head_sum", (8,) + BLOCK, F32),
    ("ent_stage", (4,) + BLOCK, BF),
    ("ent_sib", (4,) + BLOCK, BF),
    ("ent_sum", (4,) + BLOCK, BF),
    ("ent_far", (4,) + BLOCK, BF),
    ("ent_end", (8,) + BLOCK, BF),
    ("fin", (256, 512), BF),
    ("parts", (8, SLOT, 512), BF),
)
SEMAPHORES = (
    ("a", (8,)), ("i", (2,)), ("p", (2, 3)), ("z", (2, 2, 5)), ("x", (2, 8)), ("s", (16,)),
    ("n", (2, 3)), ("t", (16,)), ("w", (2, 8)), ("v", (2, 2, 4)),
    ("es", (4,)), ("ef", (4,)), ("ee", (4,)), ("c", (8,)), ("o", (9,)),
)


class Held:
    pass


def step_kernel(
    entity_in, entity_state, relation, heads, tails, negs, relation_ids, rel_out, ent_out, state_out, *scratch
):
    m = Held()
    names = [name for name, _, _ in BUFFERS]
    for name, _ in SEMAPHORES:
        names += [name + "_send", name + "_recv"]
    for name, ref in zip(names, scratch, strict=True):
        setattr(m, name, ref)
    at = Place()
    top, low = pl.ds(0, CUT), pl.ds(CUT, D - CUT)
    halves = (top, low)
    barrier = greet(at)
    load = pltpu.make_async_copy(entity_in, m.entity, m.o_recv.at[8])
    load.start()

    m.pad[...] = jnp.zeros_like(m.pad)
    m.pad[:OWN_REL, :D] = relation[...]
    m.shard[...] = m.pad[...].astype(BF)
    for b in range(2):
        m.ids_out[b, :, :EDGES] = jnp.broadcast_to(tails[b:b + 1, :], (8, EDGES))
        m.ids_out[b, :, EDGES:] = jnp.broadcast_to(negs[b], (8, NEG))
    ids = relation_ids[...]
    m.rels[...] = ids + (SLOT - OWN_REL) * ((ids * 36158) >> 20)
    pl.semaphore_wait(barrier, 21)

    slot = lax.rem(at.y, 2) * 4 + at.e
    here = at.c == at.y // 2
    mine = m.gath.at[pl.ds(pl.multiple_of(slot * SLOT, SLOT), SLOT), :]
    for k in range(8):
        y, xh = lax.rem(at.y + k // 2, 4), lax.rem(at.xh + k % 2, 2)
        peer = at.group(y, xh * 2 + at.y // 2)
        if k == 0:
            @pl.when(here)
            def _():
                pltpu.make_async_copy(m.shard, mine, m.a_recv.at[slot]).start()

            @pl.when(jnp.logical_not(here))
            def _():
                send(m.shard, mine, m.a_send.at[0], m.a_recv.at[slot], peer)
        else:
            send(m.shard, mine, m.a_send.at[k], m.a_recv.at[slot], peer)
    for b, peer in enumerate((at.next, at.prev)):
        send(m.ids_out.at[b], m.ids.at[b], m.i_send.at[b], m.i_recv.at[b], peer)
    load.wait()
    m.own[...] = m.entity[...].astype(BF)

    for k in range(8):
        settle(m.gath.at[pl.ds(k * SLOT, SLOT), :], m.a_recv.at[k])
    m.table[at.block(at.xl, 0, at.c)] = m.gath[...].astype(F32).T[:D].astype(BF)

    def ring_block(j, part):
        return m.table.at[at.incoming(j, at.xl, at.c), halves[part], :]

    def along_z(j, way, step, part):
        ref = ring_block(j, part)
        send(ref, ref, m.z_send.at[part, way, step], m.z_recv.at[part, way, step], at.along_z(way))

    def along_x(j, part):
        ref = ring_block(j, part)
        send(ref, ref, m.x_send.at[part, j], m.x_recv.at[part, j], (at.x_up, at.x_down)[part])

    def to_sibling(j, xl, q):
        ref = m.table.at[at.incoming(j, xl, at.c)]
        send(ref, ref, m.s_send.at[q], m.s_recv.at[q], at.sibling)

    for part in range(2):
        along_z(0, 0, 0, part)
        along_z(0, 1, 0, part)
        along_x(0, part)
    to_sibling(0, at.xl, 0)

    for b in range(2):
        settle(m.ids.at[b], m.i_recv.at[b])

    @pl.loop(0, 6)
    def _(t):
        b, n = t // 3, t % 3
        m.served[b, n] = dot(m.own[...], onehot(m.ids[b, 0:1, lanes(n)], 0, ROWS)).astype(BF)
        send(
            m.served.at[b, n], m.picked.at[b, n], m.p_send.at[b, n], m.p_recv.at[b, n],
            (lax.rem(at.d + 63 + 2 * b, 64), at.e),
        )

    m.rel_vec[...] = jnp.zeros_like(m.rel_vec)

    def head_rows(t):
        m.head_vec[:, lanes(t)] = dot(
            m.own[...], onehot(heads[pl.ds(t // 2, 1), lanes(t % 2)], 0, ROWS)
        )

    def absorb(k, xl, q):
        settle(m.table.at[at.incoming(k, xl, 1 - at.c)], m.s_recv.at[q])
        n, other = at.incoming(k, xl, 0), at.incoming(k, xl, 1)
        for b in range(2):
            m.rel_vec[:, b * EDGES:(b + 1) * EDGES] += dot(
                m.table[n], onehot(m.rels[b:b + 1, :], n * 256, 256)
            ) + dot(m.table[other], onehot(m.rels[b:b + 1, :], other * 256, 256))

    @pl.loop(1, 12)
    def _(j):
        way, step = at.ring_way(j), at.ring_step(j)
        split = jnp.logical_and(at.even, j == 7)
        for part in range(2):
            @pl.when(jnp.logical_and(j <= 7, jnp.logical_not(split)))
            def _():
                settle(ring_block(j, part), m.z_recv.at[part, way, step])

            @pl.when(split)
            def _():
                settle(ring_block(j, part), m.z_recv.at[part, part, 3])

            @pl.when(jnp.logical_and(j <= 6, at.ring_sent(way, step + 1, part)))
            def _():
                along_z(j, way, step + 1, part)

            @pl.when(j <= 7)
            def _():
                along_x(j, part)

        @pl.when(j <= 7)
        def _():
            to_sibling(j, at.xl, j)

        @pl.when(jnp.logical_and(j >= 2, j <= 9))
        def _():
            for part in range(2):
                settle(
                    m.table.at[at.incoming(j - 2, 1 - at.xl, at.c), halves[part], :],
                    m.x_recv.at[part, j - 2],
                )
            to_sibling(j - 2, 1 - at.xl, 6 + j)

        @pl.when(j <= 4)
        def _():
            head_rows(j - 1)

        @pl.when(jnp.logical_and(j >= 2, j <= 9))
        def _():
            absorb(j - 2, at.xl, j - 2)

        @pl.when(j >= 4)
        def _():
            absorb(j - 4, 1 - at.xl, 4 + j)

    kept = []
    for b in range(2):
        for n in range(3):
            settle(m.picked.at[b, n], m.p_recv.at[b, n])
        span = slice(b * EDGES, (b + 1) * EDGES)
        h_re, h_im = m.head_vec[:HALF, span], m.head_vec[HALF:, span]
        r_re, r_im = m.rel_vec[:HALF, span], m.rel_vec[HALF:, span]
        q = jnp.concatenate([h_re * r_re - h_im * r_im, h_re * r_im + h_im * r_re], axis=0)
        q_low = q.astype(BF)
        tail = jnp.concatenate([m.picked[b, 0], m.picked[b, 1]], axis=1).astype(F32)
        positive = jnp.sum(q * tail, axis=0, keepdims=True)
        slope = -jax.nn.sigmoid(-positive)
        scores = dot(m.picked[b, 2], q_low, ((0,), (0,)))
        neg_slope = jax.nn.sigmoid(scores).astype(BF)
        tail_grad = (slope * q).astype(BF)
        m.pick_grad[b, 0] = tail_grad[:, :256]
        m.pick_grad[b, 1] = tail_grad[:, 256:]
        m.pick_grad[b, 2] = dot(q_low, neg_slope, ACROSS).astype(BF)
        for n in range(3):
            send(
                m.pick_grad.at[b, n], m.pick_in.at[b, n], m.n_send.at[b, n], m.n_recv.at[b, n],
                (at.next, at.prev)[b],
            )
        kept.append((slope, neg_slope))

    for b in range(2):
        span = slice(b * EDGES, (b + 1) * EDGES)
        h_re, h_im = m.head_vec[:HALF, span], m.head_vec[HALF:, span]
        r_re, r_im = m.rel_vec[:HALF, span], m.rel_vec[HALF:, span]
        slope, neg_slope = kept[b]
        tail = jnp.concatenate([m.picked[b, 0], m.picked[b, 1]], axis=1).astype(F32)
        u = slope * tail + dot(m.picked[b, 2], neg_slope)
        u_re, u_im = u[:HALF], u[HALF:]
        m.rel_grad[:, span] = jnp.concatenate(
            [u_re * h_re + u_im * h_im, u_im * h_re - u_re * h_im], axis=0
        ).astype(BF)
        m.head_grad[:, span] = jnp.concatenate(
            [u_re * r_re + u_im * r_im, u_im * r_re - u_re * r_im], axis=0
        ).astype(BF)

    def rel_block(n):
        return dot(
            m.rel_grad[:, :EDGES], onehot(m.rels[0:1, :], n * 256, 256), ACROSS
        ) + dot(m.rel_grad[:, EDGES:], onehot(m.rels[1:2, :], n * 256, 256), ACROSS)

    def swap(j, xl, q):
        m.stage[q] = rel_block(at.outgoing(j, xl, 1 - at.c)).astype(BF)
        send(m.stage.at[q], m.sib.at[q], m.t_send.at[q], m.t_recv.at[q], at.sibling)

    @pl.loop(0, 9)
    def _(j):
        @pl.when(j < 8)
        def _():
            swap(j, 1 - at.xl, j)

        @pl.when(j > 0)
        def _():
            k = j - 1
            total = rel_block(at.outgoing(k, 1 - at.xl, at.c))
            settle(m.sib.at[k], m.t_recv.at[k])
            m.xs[k] = (total + m.sib[k].astype(F32)).astype(BF)
            for side, peer in ((0, at.x_up), (1, at.x_down)):
                send(
                    m.xs.at[k, halves[side], :], m.xbuf.at[k, halves[side], :],
                    m.w_send.at[side, k], m.w_recv.at[side, k], peer,
                )

    @pl.loop(0, 8)
    def _(j):
        swap(j, at.xl, 8 + j)

    def head_part(n):
        m.head_sum[n] = dot(
            m.head_grad[:, :EDGES], onehot(heads[0:1, :], n * 256, 256), ACROSS
        ) + dot(m.head_grad[:, EDGES:], onehot(heads[1:2, :], n * 256, 256), ACROSS)

    def entity_block(n):
        total = m.head_sum[n]
        for b in range(2):
            for i in range(3):
                ids = m.ids[b, 0:1, i * 256:(i + 1) * 256]
                total = total + dot(m.pick_in[b, i], onehot(ids, n * 256, 256), ACROSS)
        return total

    def entity_swap(k):
        m.ent_stage[k] = entity_block((1 - at.c) * 4 + k).astype(BF)
        send(m.ent_stage.at[k], m.ent_sib.at[k], m.es_send.at[k], m.es_recv.at[k], at.sibling)

    def entity_far(k):
        total = entity_block(at.c * 4 + k)
        settle(m.ent_sib.at[k], m.es_recv.at[k])
        m.ent_sum[k] = (total + m.ent_sib[k].astype(F32)).astype(BF)
        send(m.ent_sum.at[k], m.ent_far.at[k], m.ef_send.at[k], m.ef_recv.at[k], at.far)

    @pl.loop(0, 8)
    def _(j):
        total = rel_block(at.outgoing(j, at.xl, at.c))
        settle(m.sib.at[8 + j], m.t_recv.at[8 + j])
        for side in range(2):
            settle(m.xbuf.at[j, halves[side], :], m.w_recv.at[side, j])
        m.acc[...] = total + m.sib[8 + j].astype(F32) + m.xbuf[j].astype(F32)
        way, step = (j + 1) % 2, (j + 1) // 2

        for part in range(2):
            rows = (slice(0, CUT), slice(CUT, D))[part]

            def add(side, last):
                settle(m.zbuf.at[side, last, halves[part], :], m.v_recv.at[part, side, last])
                m.acc[rows, :] += m.zbuf[side, last, rows, :].astype(F32)

            @pl.when(jnp.logical_or(j == part + 1, jnp.logical_and(j >= 3, j <= 6)))
            def _():
                add(way, step - 1)

            @pl.when(j == 7)
            def _():
                add(0, 3)
                add(1, 3)

            @pl.when(j <= 6)
            def _():
                m.zs[j, rows, :] = m.acc[rows, :].astype(BF)
                side = jnp.where(j == 0, part, way)
                send(
                    m.zs.at[j, halves[part], :], m.zbuf.at[side, step, halves[part], :],
                    m.v_send.at[part, side, step], m.v_recv.at[part, side, step], at.along_z(side),
                )

        @pl.when(j < 4)
        def _():
            head_part(2 * j)
            head_part(2 * j + 1)

        @pl.when(j == 4)
        def _():
            for b in range(2):
                for n in range(3):
                    settle(m.pick_in.at[b, n], m.n_recv.at[b, n])

            @pl.loop(0, 5)
            def _(i):
                @pl.when(i < 4)
                def _():
                    entity_swap(i)

                @pl.when(i > 0)
                def _():
                    entity_far(i - 1)

    m.fin[...] = jnp.concatenate([m.acc[...], jnp.zeros((512 - D, 256), F32)], axis=0).T.astype(BF)
    source = at.y * 2 + at.xh
    for k in range(8):
        y, e = 2 * at.c + k // 4, k % 4
        mine_too = jnp.logical_and(at.y == y, at.e == e)
        piece = m.fin.at[pl.ds(k * SLOT, SLOT), :]

        @pl.when(mine_too)
        def _():
            pltpu.make_async_copy(piece, m.parts.at[source], m.c_recv.at[source]).start()

        @pl.when(jnp.logical_not(mine_too))
        def _():
            send(piece, m.parts.at[source], m.c_send.at[k], m.c_recv.at[source], at.group(y, e))

    @pl.loop(0, 4)
    def _(k):
        settle(m.ent_far.at[k], m.ef_recv.at[k])
        n = at.c * 4 + k
        m.ent_end[n] = (m.ent_sum[k].astype(F32) + m.ent_far[k].astype(F32)).astype(BF)
        send(m.ent_end.at[n], m.ent_end.at[n], m.ee_send.at[k], m.ee_recv.at[k], at.sibling)

    for k in range(8):
        settle(m.parts.at[k], m.c_recv.at[k])
    rel_out[...] = jnp.sum(m.parts[...].astype(F32), axis=0)
    def adagrad(n):
        grad = m.ent_end[n].astype(F32)
        history = entity_state[:, lanes(n)] + jnp.sum(grad * grad, axis=0, keepdims=True) * (1.0 / D)
        state_out[:, lanes(n)] = history
        m.entity[:, lanes(n)] -= grad * (LEARN_RATE / jnp.sqrt(history))
        pltpu.make_async_copy(m.entity.at[:, lanes(n)], ent_out.at[:, lanes(n)], m.o_recv.at[n]).start()

    @pl.loop(0, 4)
    def _(k):
        adagrad(at.c * 4 + k)

    @pl.loop(0, 4)
    def _(k):
        settle(m.ent_end.at[(1 - at.c) * 4 + k], m.ee_recv.at[k])
        adagrad((1 - at.c) * 4 + k)

    for n in range(8):
        pltpu.make_async_copy(m.entity.at[:, lanes(n)], ent_out.at[:, lanes(n)], m.o_recv.at[n]).wait()

    @pl.when(jnp.logical_not(here))
    def _():
        settle(m.shard, m.a_send.at[0])

    for k in range(1, 8):
        settle(m.shard, m.a_send.at[k])
    for k in range(8):
        y, e = 2 * at.c + k // 4, k % 4

        @pl.when(jnp.logical_not(jnp.logical_and(at.y == y, at.e == e)))
        def _():
            settle(m.parts.at[0], m.c_send.at[k])

    one = m.stage.at[0]
    for b in range(2):
        settle(m.ids_out.at[b], m.i_send.at[b])
        for n in range(3):
            settle(one, m.p_send.at[b, n])
            settle(one, m.n_send.at[b, n])
        half = m.stage.at[0, halves[b], :]
        for way in range(2):
            for step in range(5):
                @pl.when(at.ring_sent(way, step, b))
                def _():
                    settle(half, m.z_send.at[b, way, step])

            for step in range(3):
                settle(half, m.v_send.at[b, way, step + 1])
        settle(half, m.v_send.at[b, b, 0])
        for j in range(8):
            settle(half, m.x_send.at[b, j])
            settle(half, m.w_send.at[b, j])
    for q in range(16):
        settle(one, m.s_send.at[q])
        settle(one, m.t_send.at[q])
    for k in range(4):
        settle(one, m.es_send.at[k])
        settle(one, m.ef_send.at[k])
        settle(one, m.ee_send.at[k])


def whole_step(entity, entity_state, relation, heads, tails, negs, relation_ids):
    vmem = pl.BlockSpec(memory_space=pltpu.VMEM)
    anywhere = pl.BlockSpec(memory_space=pl.ANY)
    scratch = [pltpu.VMEM(shape, kind) for _, shape, kind in BUFFERS]
    for _, shape in SEMAPHORES:
        scratch += [DMA(shape), DMA(shape)]
    return pl.pallas_call(
        step_kernel,
        out_shape=(
            jax.ShapeDtypeStruct((SLOT, 512), F32),
            jax.ShapeDtypeStruct((D, ROWS), F32),
            jax.ShapeDtypeStruct((1, ROWS), F32),
        ),
        in_specs=[anywhere] + [vmem] * 6,
        out_specs=(vmem, anywhere, vmem),
        scratch_shapes=scratch,
        compiler_params=pltpu.CompilerParams(
            collective_id=0, has_side_effects=True, vmem_limit_bytes=60 * MIB
        ),
        name="whole_step",
    )(entity, entity_state, relation, heads, tails, negs, relation_ids)


def local(
    entity_emb,
    entity_state,
    relation_emb,
    relation_state,
    head_rows,
    tail_rows,
    relation_ids,
    negative_rows,
):
    relation_grad, new_entity, new_entity_state = whole_step(
        entity_emb.T, entity_state[None], relation_emb, head_rows, tail_rows, negative_rows, relation_ids
    )
    relation_grad = relation_grad[:OWN_REL, :D]
    new_relation_state = relation_state + jnp.mean(relation_grad * relation_grad, axis=-1)
    new_relation_emb = relation_emb - LEARN_RATE * relation_grad / jnp.sqrt(new_relation_state)[:, None]
    return (new_entity.T, new_entity_state[0], new_relation_emb, new_relation_state)


def solution(mesh):
    placed = (
        P("dom", None),
        P("dom"),
        P(("dom", "edge"), None),
        P(("dom", "edge")),
        P(None, ("dom", "edge")),
        P(None, ("dom", "edge")),
        P(None, ("dom", "edge")),
        P(None, ("dom", "edge"), None),
    )
    return jax.shard_map(
        local,
        mesh=mesh,
        in_specs=placed,
        out_specs=(P("dom", None), P("dom"), P(("dom", "edge"), None), P(("dom", "edge"))),
        check_vma=False,
    )
```

```python
import jax
import jax.numpy as jnp
from jax import lax
from jax.experimental import pallas as pl
from jax.experimental.pallas import tpu as pltpu
from jax.sharding import PartitionSpec as P

LEARN_RATE = 0.5
D = 400
HALF = 200
ROWS = 2048
EDGES = 512
NEG = 256
PICKS = EDGES + NEG
OWN_REL = 29
SLOT = 32
CUT = 208
Z = 8
BLOCKS = 32
MIB = 1 << 20
MESH = pl.DeviceIdType.MESH
BF = jnp.bfloat16
F32 = jnp.float32
ACROSS = ((1,), (1,))


class Place:
    def __init__(self):
        self.d = lax.axis_index("dom")
        self.e = lax.axis_index("edge")
        self.y = lax.rem(self.d, 4)
        self.z = lax.rem(self.d // 4, Z)
        self.xl = self.d // 32
        self.even = jnp.logical_and(self.y > 0, self.y < 3)
        self.xh = self.e // 2
        self.c = lax.rem(self.e, 2)
        x = self.xh * 2 + self.xl
        other = lax.rem(self.d + 32, 64)
        self.x_up = (other, (lax.rem(x + 1, 4) // 2) * 2 + self.c)
        self.x_down = (other, (lax.rem(x + 3, 4) // 2) * 2 + self.c)
        self.z_up = self.along_z(0)
        self.z_down = self.along_z(1)
        self.next = (lax.rem(self.d + 1, 64), self.e)
        self.prev = (lax.rem(self.d + 63, 64), self.e)
        self.sibling = (self.d, self.xh * 2 + 1 - self.c)
        self.far = (self.d, (1 - self.xh) * 2 + self.c)

    def along_z(self, way):
        return (self.xl * 32 + lax.rem(self.z + 1 + 6 * way, Z) * 4 + self.y, self.e)

    def group(self, y, e):
        return (self.d - self.y + y, e)

    def block(self, xl, offset, half):
        return (xl * Z + lax.rem(self.z + offset + Z, Z)) * 2 + half

    def ring_step(self, j):
        return (jnp.where(self.even, 0x32211000, 0x43121000) >> (4 * jnp.minimum(j, 7))) & 15

    def ring_way(self, j):
        return (jnp.where(self.even, 0x54, jnp.where(self.y == 0, 0x24, 0xDA)) >> j) & 1

    def ring_sent(self, way, step, part):
        most = jnp.where(self.even, jnp.where(part == way, 4, 3), jnp.where(way == self.y // 3, 5, 2))
        return step < most

    def incoming(self, j, xl, half):
        away = self.ring_step(j) + 1
        away = jnp.where(self.ring_way(j) == 1, away, -away)
        return self.block(xl, jnp.where(j == 0, 0, away), half)

    def outgoing(self, j, xl, half):
        away = 4 - (j + 1) // 2
        return self.block(xl, jnp.where(j % 2 == 1, away, -away), half)


def greet(at):
    barrier = pltpu.get_barrier_semaphore()
    where = at.y * 4 + at.e
    for k in range(1, 16):
        peer = lax.rem(where + k, 16)
        pl.semaphore_signal(
            barrier, inc=1, device_id=at.group(peer // 4, lax.rem(peer, 4)), device_id_type=MESH
        )
    for peer in (at.x_up, at.x_down, at.z_up, at.z_down, at.next, at.prev):
        pl.semaphore_signal(barrier, inc=1, device_id=peer, device_id_type=MESH)
    return barrier


def send(src, dst, send_sem, recv_sem, peer):
    pltpu.make_async_remote_copy(
        src_ref=src,
        dst_ref=dst,
        send_sem=send_sem,
        recv_sem=recv_sem,
        device_id=peer,
        device_id_type=MESH,
    ).start()


def settle(ref, sem):
    pltpu.make_async_copy(ref, ref, sem).wait()


def onehot(ids, base, rows):
    at = lax.broadcasted_iota(jnp.int32, (rows, ids.shape[1]), 0) + base
    return jnp.where(at == ids, 1.0, 0.0).astype(BF)


def columns(ids):
    return jnp.broadcast_to(ids, (128, ids.shape[1])).T


def spread(cols, bases):
    lane = lax.broadcasted_iota(jnp.int32, cols.shape, 1)
    tiles = []
    for base in bases:
        for k in (0, 128):
            tiles.append(jnp.where(cols - (base + k) == lane, 1.0, 0.0).astype(BF))
    return jnp.concatenate(tiles, axis=1)


def dot(a, b, over=((1,), (0,))):
    return lax.dot_general(a, b, (over, ((), ())), preferred_element_type=F32)


def lanes(k):
    return pl.ds(pl.multiple_of(k * 256, 256), 256)


BLOCK = (D, 256)
DMA = pltpu.SemaphoreType.DMA
BUFFERS = (
    ("entity", (D, ROWS), F32),
    ("pad", (SLOT, 512), F32),
    ("shard", (SLOT, 512), BF),
    ("own", (D, ROWS), BF),
    ("rels", (2, EDGES), jnp.int32),
    ("ids_out", (2, 8, PICKS), jnp.int32),
    ("ids", (2, 8, PICKS), jnp.int32),
    ("gath", (256, 512), BF),
    ("table", (BLOCKS,) + BLOCK, BF),
    ("served", (2, 3) + BLOCK, BF),
    ("picked", (2, 3) + BLOCK, BF),
    ("head_vec", (D, 2 * EDGES), F32),
    ("rel_vec", (D, 2 * EDGES), F32),
    ("head_grad", (D, 2 * EDGES), BF),
    ("rel_grad", (D, 2 * EDGES), BF),
    ("pick_grad", (2, 3) + BLOCK, BF),
    ("pick_in", (2, 3) + BLOCK, BF),
    ("stage", (16,) + BLOCK, BF),
    ("sib", (16,) + BLOCK, BF),
    ("xs", (8,) + BLOCK, BF),
    ("xbuf", (8,) + BLOCK, BF),
    ("rel_cols", (2 * EDGES, 128), jnp.int32),
    ("head_cols", (2 * EDGES, 128), jnp.int32),
    ("pick_cols", (2 * PICKS, 128), jnp.int32),
    ("beside", (2,) + BLOCK, F32),
    ("within", (8,) + BLOCK, F32),
    ("acc", BLOCK, F32),
    ("zs", (7,) + BLOCK, BF),
    ("zbuf", (2, 4) + BLOCK, BF),
    ("head_sum", (8,) + BLOCK, F32),
    ("ent_stage", (4,) + BLOCK, BF),
    ("ent_sib", (4,) + BLOCK, BF),
    ("ent_sum", (4,) + BLOCK, BF),
    ("ent_far", (4,) + BLOCK, BF),
    ("ent_end", (8,) + BLOCK, BF),
    ("fin", (256, 512), BF),
    ("parts", (8, SLOT, 512), BF),
)
SEMAPHORES = (
    ("a", (8,)), ("i", (2,)), ("p", (2, 3)), ("z", (2, 2, 5)), ("x", (2, 8)), ("s", (16,)),
    ("n", (2, 3)), ("t", (16,)), ("w", (2, 8)), ("v", (2, 2, 4)),
    ("es", (4,)), ("ef", (4,)), ("ee", (4,)), ("c", (8,)), ("o", (9,)),
)


class Held:
    pass


def step_kernel(
    entity_in, entity_state, relation, heads, tails, negs, relation_ids, rel_out, ent_out, state_out, *scratch
):
    m = Held()
    names = [name for name, _, _ in BUFFERS]
    for name, _ in SEMAPHORES:
        names += [name + "_send", name + "_recv"]
    for name, ref in zip(names, scratch, strict=True):
        setattr(m, name, ref)
    at = Place()
    top, low = pl.ds(0, CUT), pl.ds(CUT, D - CUT)
    halves = (top, low)
    barrier = greet(at)
    load = pltpu.make_async_copy(entity_in, m.entity, m.o_recv.at[8])
    load.start()

    m.pad[...] = jnp.zeros_like(m.pad)
    m.pad[:OWN_REL, :D] = relation[...]
    m.shard[...] = m.pad[...].astype(BF)
    for b in range(2):
        m.ids_out[b, :, :EDGES] = jnp.broadcast_to(tails[b:b + 1, :], (8, EDGES))
        m.ids_out[b, :, EDGES:] = jnp.broadcast_to(negs[b], (8, NEG))
    ids = relation_ids[...]
    m.rels[...] = ids + (SLOT - OWN_REL) * ((ids * 36158) >> 20)
    pl.semaphore_wait(barrier, 21)

    slot = lax.rem(at.y, 2) * 4 + at.e
    here = at.c == at.y // 2
    mine = m.gath.at[pl.ds(pl.multiple_of(slot * SLOT, SLOT), SLOT), :]
    for k in range(8):
        y, xh = lax.rem(at.y + k // 2, 4), lax.rem(at.xh + k % 2, 2)
        peer = at.group(y, xh * 2 + at.y // 2)
        if k == 0:
            @pl.when(here)
            def _():
                pltpu.make_async_copy(m.shard, mine, m.a_recv.at[slot]).start()

            @pl.when(jnp.logical_not(here))
            def _():
                send(m.shard, mine, m.a_send.at[0], m.a_recv.at[slot], peer)
        else:
            send(m.shard, mine, m.a_send.at[k], m.a_recv.at[slot], peer)
    for b, peer in enumerate((at.next, at.prev)):
        send(m.ids_out.at[b], m.ids.at[b], m.i_send.at[b], m.i_recv.at[b], peer)
    load.wait()
    m.own[...] = m.entity[...].astype(BF)
    for b in range(2):
        m.rel_cols[b * EDGES:(b + 1) * EDGES, :] = columns(m.rels[b:b + 1, :])
        m.head_cols[b * EDGES:(b + 1) * EDGES, :] = columns(heads[b:b + 1, :])

    for k in range(8):
        settle(m.gath.at[pl.ds(k * SLOT, SLOT), :], m.a_recv.at[k])
    m.table[at.block(at.xl, 0, at.c)] = m.gath[...].astype(F32).T[:D].astype(BF)

    def ring_block(j, part):
        return m.table.at[at.incoming(j, at.xl, at.c), halves[part], :]

    def along_z(j, way, step, part):
        ref = ring_block(j, part)
        send(ref, ref, m.z_send.at[part, way, step], m.z_recv.at[part, way, step], at.along_z(way))

    def along_x(j, part):
        ref = ring_block(j, part)
        send(ref, ref, m.x_send.at[part, j], m.x_recv.at[part, j], (at.x_up, at.x_down)[part])

    def to_sibling(j, xl, q):
        ref = m.table.at[at.incoming(j, xl, at.c)]
        send(ref, ref, m.s_send.at[q], m.s_recv.at[q], at.sibling)

    for part in range(2):
        along_z(0, 0, 0, part)
        along_z(0, 1, 0, part)
        along_x(0, part)
    to_sibling(0, at.xl, 0)

    for b in range(2):
        settle(m.ids.at[b], m.i_recv.at[b])

    @pl.loop(0, 6)
    def _(t):
        b, n = t // 3, t % 3
        m.served[b, n] = dot(m.own[...], onehot(m.ids[b, 0:1, lanes(n)], 0, ROWS)).astype(BF)
        send(
            m.served.at[b, n], m.picked.at[b, n], m.p_send.at[b, n], m.p_recv.at[b, n],
            (lax.rem(at.d + 63 + 2 * b, 64), at.e),
        )

    for b in range(2):
        m.pick_cols[b * PICKS:(b + 1) * PICKS, :] = columns(m.ids[b, 0:1, :])
    m.rel_vec[...] = jnp.zeros_like(m.rel_vec)

    def head_rows(t):
        m.head_vec[:, lanes(t)] = dot(
            m.own[...], onehot(heads[pl.ds(t // 2, 1), lanes(t % 2)], 0, ROWS)
        )

    def absorb(k, xl, q):
        settle(m.table.at[at.incoming(k, xl, 1 - at.c)], m.s_recv.at[q])
        n, other = at.incoming(k, xl, 0), at.incoming(k, xl, 1)
        for b in range(2):
            m.rel_vec[:, b * EDGES:(b + 1) * EDGES] += dot(
                m.table[n], onehot(m.rels[b:b + 1, :], n * 256, 256)
            ) + dot(m.table[other], onehot(m.rels[b:b + 1, :], other * 256, 256))

    @pl.loop(1, 12)
    def _(j):
        way, step = at.ring_way(j), at.ring_step(j)
        split = jnp.logical_and(at.even, j == 7)
        for part in range(2):
            @pl.when(jnp.logical_and(j <= 7, jnp.logical_not(split)))
            def _():
                settle(ring_block(j, part), m.z_recv.at[part, way, step])

            @pl.when(split)
            def _():
                settle(ring_block(j, part), m.z_recv.at[part, part, 3])

            @pl.when(jnp.logical_and(j <= 6, at.ring_sent(way, step + 1, part)))
            def _():
                along_z(j, way, step + 1, part)

            @pl.when(j <= 7)
            def _():
                along_x(j, part)

        @pl.when(j <= 7)
        def _():
            to_sibling(j, at.xl, j)

        @pl.when(jnp.logical_and(j >= 2, j <= 9))
        def _():
            for part in range(2):
                settle(
                    m.table.at[at.incoming(j - 2, 1 - at.xl, at.c), halves[part], :],
                    m.x_recv.at[part, j - 2],
                )
            to_sibling(j - 2, 1 - at.xl, 6 + j)

        @pl.when(j <= 4)
        def _():
            head_rows(j - 1)

        @pl.when(jnp.logical_and(j >= 2, j <= 9))
        def _():
            absorb(j - 2, at.xl, j - 2)

        @pl.when(j >= 4)
        def _():
            absorb(j - 4, 1 - at.xl, 4 + j)

    kept = []
    for b in range(2):
        for n in range(3):
            settle(m.picked.at[b, n], m.p_recv.at[b, n])
        span = slice(b * EDGES, (b + 1) * EDGES)
        h_re, h_im = m.head_vec[:HALF, span], m.head_vec[HALF:, span]
        r_re, r_im = m.rel_vec[:HALF, span], m.rel_vec[HALF:, span]
        q = jnp.concatenate([h_re * r_re - h_im * r_im, h_re * r_im + h_im * r_re], axis=0)
        q_low = q.astype(BF)
        tail = jnp.concatenate([m.picked[b, 0], m.picked[b, 1]], axis=1).astype(F32)
        positive = jnp.sum(q * tail, axis=0, keepdims=True)
        slope = -jax.nn.sigmoid(-positive)
        scores = dot(m.picked[b, 2], q_low, ((0,), (0,)))
        neg_slope = jax.nn.sigmoid(scores).astype(BF)
        tail_grad = (slope * q).astype(BF)
        m.pick_grad[b, 0] = tail_grad[:, :256]
        m.pick_grad[b, 1] = tail_grad[:, 256:]
        m.pick_grad[b, 2] = dot(q_low, neg_slope, ACROSS).astype(BF)
        for n in range(3):
            send(
                m.pick_grad.at[b, n], m.pick_in.at[b, n], m.n_send.at[b, n], m.n_recv.at[b, n],
                (at.next, at.prev)[b],
            )
        kept.append((slope, neg_slope))

    for b in range(2):
        span = slice(b * EDGES, (b + 1) * EDGES)
        h_re, h_im = m.head_vec[:HALF, span], m.head_vec[HALF:, span]
        r_re, r_im = m.rel_vec[:HALF, span], m.rel_vec[HALF:, span]
        slope, neg_slope = kept[b]
        tail = jnp.concatenate([m.picked[b, 0], m.picked[b, 1]], axis=1).astype(F32)
        u = slope * tail + dot(m.picked[b, 2], neg_slope)
        u_re, u_im = u[:HALF], u[HALF:]
        m.rel_grad[:, span] = jnp.concatenate(
            [u_re * h_re + u_im * h_im, u_im * h_re - u_re * h_im], axis=0
        ).astype(BF)
        m.head_grad[:, span] = jnp.concatenate(
            [u_re * r_re + u_im * r_im, u_im * r_re - u_re * r_im], axis=0
        ).astype(BF)

    def rel_pair(j, xl, q):
        mine, other = at.outgoing(j, xl, at.c), at.outgoing(j, xl, 1 - at.c)
        pair = dot(m.rel_grad[...], spread(m.rel_cols[...], (mine * 256, other * 256)))
        m.stage[q] = pair[:, 256:].astype(BF)
        send(m.stage.at[q], m.sib.at[q], m.t_send.at[q], m.t_recv.at[q], at.sibling)
        return pair[:, :256]

    def to_x(k):
        settle(m.sib.at[k], m.t_recv.at[k])
        m.xs[k] = (m.beside[k % 2] + m.sib[k].astype(F32)).astype(BF)
        for side, peer in ((0, at.x_up), (1, at.x_down)):
            send(
                m.xs.at[k, halves[side], :], m.xbuf.at[k, halves[side], :],
                m.w_send.at[side, k], m.w_recv.at[side, k], peer,
            )

    def head_pair(k):
        pair = dot(m.head_grad[...], spread(m.head_cols[...], (k * 512, k * 512 + 256)))
        m.head_sum[2 * k] = pair[:, :256]
        m.head_sum[2 * k + 1] = pair[:, 256:]

    def entity_pair(k):
        total = None
        for b in range(2):
            for i in range(3):
                start = b * PICKS + i * 256
                term = dot(
                    m.pick_in[b, i],
                    spread(m.pick_cols[start:start + 256, :], (k * 512, k * 512 + 256)),
                )
                total = term if total is None else total + term
        m.head_sum[2 * k] += total[:, :256]
        m.head_sum[2 * k + 1] += total[:, 256:]

    def entity_swap(k):
        m.ent_stage[k] = m.head_sum[(1 - at.c) * 4 + k].astype(BF)
        send(m.ent_stage.at[k], m.ent_sib.at[k], m.es_send.at[k], m.es_recv.at[k], at.sibling)

    def entity_far(k):
        settle(m.ent_sib.at[k], m.es_recv.at[k])
        m.ent_sum[k] = (m.head_sum[at.c * 4 + k] + m.ent_sib[k].astype(F32)).astype(BF)
        send(m.ent_sum.at[k], m.ent_far.at[k], m.ef_send.at[k], m.ef_recv.at[k], at.far)

    def z_step(j):
        settle(m.sib.at[8 + j], m.t_recv.at[8 + j])
        for side in range(2):
            settle(m.xbuf.at[j, halves[side], :], m.w_recv.at[side, j])
        m.acc[...] = m.within[j] + m.sib[8 + j].astype(F32) + m.xbuf[j].astype(F32)
        way, step = (j + 1) % 2, (j + 1) // 2

        for part in range(2):
            rows = (slice(0, CUT), slice(CUT, D))[part]

            def add(side, last):
                settle(m.zbuf.at[side, last, halves[part], :], m.v_recv.at[part, side, last])
                m.acc[rows, :] += m.zbuf[side, last, rows, :].astype(F32)

            @pl.when(jnp.logical_or(j == part + 1, jnp.logical_and(j >= 3, j <= 6)))
            def _():
                add(way, step - 1)

            @pl.when(j == 7)
            def _():
                add(0, 3)
                add(1, 3)

            @pl.when(j <= 6)
            def _():
                m.zs[j, rows, :] = m.acc[rows, :].astype(BF)
                side = jnp.where(j == 0, part, way)
                send(
                    m.zs.at[j, halves[part], :], m.zbuf.at[side, step, halves[part], :],
                    m.v_send.at[part, side, step], m.v_recv.at[part, side, step], at.along_z(side),
                )

    @pl.loop(0, 11)
    def _(j):
        @pl.when(j < 8)
        def _():
            m.beside[j % 2] = rel_pair(j, 1 - at.xl, j)

        @pl.when(jnp.logical_and(j >= 1, j <= 8))
        def _():
            to_x(j - 1)

        @pl.when(j < 8)
        def _():
            m.within[j] = rel_pair(j, at.xl, 8 + j)

        @pl.when(jnp.logical_and(j >= 4, j <= 7))
        def _():
            head_pair(j - 4)

        @pl.when(j >= 3)
        def _():
            z_step(j - 3)

        @pl.when(j == 8)
        def _():
            for b in range(2):
                for n in range(3):
                    settle(m.pick_in.at[b, n], m.n_recv.at[b, n])

            @pl.loop(0, 2)
            def _(i):
                entity_pair((1 - at.c) * 2 + i)
                entity_swap(2 * i)
                entity_swap(2 * i + 1)

            @pl.loop(0, 2)
            def _(i):
                entity_pair(at.c * 2 + i)
                entity_far(2 * i)
                entity_far(2 * i + 1)

    m.fin[...] = jnp.concatenate([m.acc[...], jnp.zeros((512 - D, 256), F32)], axis=0).T.astype(BF)
    source = at.y * 2 + at.xh
    for k in range(8):
        y, e = 2 * at.c + k // 4, k % 4
        mine_too = jnp.logical_and(at.y == y, at.e == e)
        piece = m.fin.at[pl.ds(k * SLOT, SLOT), :]

        @pl.when(mine_too)
        def _():
            pltpu.make_async_copy(piece, m.parts.at[source], m.c_recv.at[source]).start()

        @pl.when(jnp.logical_not(mine_too))
        def _():
            send(piece, m.parts.at[source], m.c_send.at[k], m.c_recv.at[source], at.group(y, e))

    @pl.loop(0, 4)
    def _(k):
        settle(m.ent_far.at[k], m.ef_recv.at[k])
        n = at.c * 4 + k
        m.ent_end[n] = (m.ent_sum[k].astype(F32) + m.ent_far[k].astype(F32)).astype(BF)
        send(m.ent_end.at[n], m.ent_end.at[n], m.ee_send.at[k], m.ee_recv.at[k], at.sibling)

    for k in range(8):
        settle(m.parts.at[k], m.c_recv.at[k])
    rel_out[...] = jnp.sum(m.parts[...].astype(F32), axis=0)
    def adagrad(n):
        grad = m.ent_end[n].astype(F32)
        history = entity_state[:, lanes(n)] + jnp.sum(grad * grad, axis=0, keepdims=True) * (1.0 / D)
        state_out[:, lanes(n)] = history
        m.entity[:, lanes(n)] -= grad * (LEARN_RATE / jnp.sqrt(history))
        pltpu.make_async_copy(m.entity.at[:, lanes(n)], ent_out.at[:, lanes(n)], m.o_recv.at[n]).start()

    @pl.loop(0, 4)
    def _(k):
        adagrad(at.c * 4 + k)

    @pl.loop(0, 4)
    def _(k):
        settle(m.ent_end.at[(1 - at.c) * 4 + k], m.ee_recv.at[k])
        adagrad((1 - at.c) * 4 + k)

    for n in range(8):
        pltpu.make_async_copy(m.entity.at[:, lanes(n)], ent_out.at[:, lanes(n)], m.o_recv.at[n]).wait()

    @pl.when(jnp.logical_not(here))
    def _():
        settle(m.shard, m.a_send.at[0])

    for k in range(1, 8):
        settle(m.shard, m.a_send.at[k])
    for k in range(8):
        y, e = 2 * at.c + k // 4, k % 4

        @pl.when(jnp.logical_not(jnp.logical_and(at.y == y, at.e == e)))
        def _():
            settle(m.parts.at[0], m.c_send.at[k])

    one = m.stage.at[0]
    for b in range(2):
        settle(m.ids_out.at[b], m.i_send.at[b])
        for n in range(3):
            settle(one, m.p_send.at[b, n])
            settle(one, m.n_send.at[b, n])
        half = m.stage.at[0, halves[b], :]
        for way in range(2):
            for step in range(5):
                @pl.when(at.ring_sent(way, step, b))
                def _():
                    settle(half, m.z_send.at[b, way, step])

            for step in range(3):
                settle(half, m.v_send.at[b, way, step + 1])
        settle(half, m.v_send.at[b, b, 0])
        for j in range(8):
            settle(half, m.x_send.at[b, j])
            settle(half, m.w_send.at[b, j])
    for q in range(16):
        settle(one, m.s_send.at[q])
        settle(one, m.t_send.at[q])
    for k in range(4):
        settle(one, m.es_send.at[k])
        settle(one, m.ef_send.at[k])
        settle(one, m.ee_send.at[k])


def whole_step(entity, entity_state, relation, heads, tails, negs, relation_ids):
    vmem = pl.BlockSpec(memory_space=pltpu.VMEM)
    anywhere = pl.BlockSpec(memory_space=pl.ANY)
    scratch = [pltpu.VMEM(shape, kind) for _, shape, kind in BUFFERS]
    for _, shape in SEMAPHORES:
        scratch += [DMA(shape), DMA(shape)]
    return pl.pallas_call(
        step_kernel,
        out_shape=(
            jax.ShapeDtypeStruct((SLOT, 512), F32),
            jax.ShapeDtypeStruct((D, ROWS), F32),
            jax.ShapeDtypeStruct((1, ROWS), F32),
        ),
        in_specs=[anywhere] + [vmem] * 6,
        out_specs=(vmem, anywhere, vmem),
        scratch_shapes=scratch,
        compiler_params=pltpu.CompilerParams(
            collective_id=0, has_side_effects=True, vmem_limit_bytes=60 * MIB
        ),
        name="whole_step",
    )(entity, entity_state, relation, heads, tails, negs, relation_ids)


def local(
    entity_emb,
    entity_state,
    relation_emb,
    relation_state,
    head_rows,
    tail_rows,
    relation_ids,
    negative_rows,
):
    relation_grad, new_entity, new_entity_state = whole_step(
        entity_emb.T, entity_state[None], relation_emb, head_rows, tail_rows, negative_rows, relation_ids
    )
    relation_grad = relation_grad[:OWN_REL, :D]
    new_relation_state = relation_state + jnp.mean(relation_grad * relation_grad, axis=-1)
    new_relation_emb = relation_emb - LEARN_RATE * relation_grad / jnp.sqrt(new_relation_state)[:, None]
    return (new_entity.T, new_entity_state[0], new_relation_emb, new_relation_state)


def solution(mesh):
    placed = (
        P("dom", None),
        P("dom"),
        P(("dom", "edge"), None),
        P(("dom", "edge")),
        P(None, ("dom", "edge")),
        P(None, ("dom", "edge")),
        P(None, ("dom", "edge")),
        P(None, ("dom", "edge"), None),
    )
    return jax.shard_map(
        local,
        mesh=mesh,
        in_specs=placed,
        out_specs=(P("dom", None), P("dom"), P(("dom", "edge"), None), P(("dom", "edge"))),
        check_vma=False,
    )
```

```python
import jax
import jax.numpy as jnp
from jax import lax
from jax.experimental import pallas as pl
from jax.experimental.pallas import tpu as pltpu
from jax.sharding import PartitionSpec as P

LEARN_RATE = 0.5
D = 400
HALF = 200
ROWS = 2048
EDGES = 512
NEG = 256
PICKS = EDGES + NEG
OWN_REL = 29
SLOT = 32
CUT = 208
Z = 8
BLOCKS = 32
MIB = 1 << 20
MESH = pl.DeviceIdType.MESH
BF = jnp.bfloat16
F32 = jnp.float32
ACROSS = ((1,), (1,))


class Place:
    def __init__(self):
        self.d = lax.axis_index("dom")
        self.e = lax.axis_index("edge")
        self.y = lax.rem(self.d, 4)
        self.z = lax.rem(self.d // 4, Z)
        self.xl = self.d // 32
        self.even = jnp.logical_and(self.y > 0, self.y < 3)
        self.xh = self.e // 2
        self.c = lax.rem(self.e, 2)
        x = self.xh * 2 + self.xl
        other = lax.rem(self.d + 32, 64)
        self.x_up = (other, (lax.rem(x + 1, 4) // 2) * 2 + self.c)
        self.x_down = (other, (lax.rem(x + 3, 4) // 2) * 2 + self.c)
        self.z_up = self.along_z(0)
        self.z_down = self.along_z(1)
        self.next = (lax.rem(self.d + 1, 64), self.e)
        self.prev = (lax.rem(self.d + 63, 64), self.e)
        self.sibling = (self.d, self.xh * 2 + 1 - self.c)
        self.far = (self.d, (1 - self.xh) * 2 + self.c)

    def along_z(self, way):
        return (self.xl * 32 + lax.rem(self.z + 1 + 6 * way, Z) * 4 + self.y, self.e)

    def group(self, y, e):
        return (self.d - self.y + y, e)

    def block(self, xl, offset, half):
        return (xl * Z + lax.rem(self.z + offset + Z, Z)) * 2 + half

    def ring_step(self, j):
        return (jnp.where(self.even, 0x32211000, 0x43121000) >> (4 * jnp.minimum(j, 7))) & 15

    def ring_way(self, j):
        return (jnp.where(self.even, 0x54, jnp.where(self.y == 0, 0x24, 0xDA)) >> j) & 1

    def ring_sent(self, way, step, part):
        most = jnp.where(self.even, jnp.where(part == way, 4, 3), jnp.where(way == self.y // 3, 5, 2))
        return step < most

    def incoming(self, j, xl, half):
        away = self.ring_step(j) + 1
        away = jnp.where(self.ring_way(j) == 1, away, -away)
        return self.block(xl, jnp.where(j == 0, 0, away), half)

    def outgoing(self, j, xl, half):
        away = 4 - (j + 1) // 2
        return self.block(xl, jnp.where(j % 2 == 1, away, -away), half)


def greet(at):
    barrier = pltpu.get_barrier_semaphore()
    where = at.y * 4 + at.e
    for k in range(1, 16):
        peer = lax.rem(where + k, 16)
        pl.semaphore_signal(
            barrier, inc=1, device_id=at.group(peer // 4, lax.rem(peer, 4)), device_id_type=MESH
        )
    for peer in (at.x_up, at.x_down, at.z_up, at.z_down, at.next, at.prev):
        pl.semaphore_signal(barrier, inc=1, device_id=peer, device_id_type=MESH)
    return barrier


def send(src, dst, send_sem, recv_sem, peer):
    pltpu.make_async_remote_copy(
        src_ref=src,
        dst_ref=dst,
        send_sem=send_sem,
        recv_sem=recv_sem,
        device_id=peer,
        device_id_type=MESH,
    ).start()


def settle(ref, sem):
    pltpu.make_async_copy(ref, ref, sem).wait()


def onehot(ids, base, rows):
    at = lax.broadcasted_iota(jnp.int32, (rows, ids.shape[1]), 0) + base
    return jnp.where(at == ids, 1.0, 0.0).astype(BF)


def columns(ids):
    return jnp.broadcast_to(ids, (128, ids.shape[1])).T


def spread(cols, bases):
    lane = lax.broadcasted_iota(jnp.int32, cols.shape, 1)
    tiles = []
    for base in bases:
        for k in (0, 128):
            tiles.append(jnp.where(cols - (base + k) == lane, 1.0, 0.0).astype(BF))
    return jnp.concatenate(tiles, axis=1)


def dot(a, b, over=((1,), (0,))):
    return lax.dot_general(a, b, (over, ((), ())), preferred_element_type=F32)


def lanes(k):
    return pl.ds(pl.multiple_of(k * 256, 256), 256)


BLOCK = (D, 256)
DMA = pltpu.SemaphoreType.DMA
BUFFERS = (
    ("entity", (D, ROWS), F32),
    ("pad", (SLOT, 512), F32),
    ("shard", (SLOT, 512), BF),
    ("own", (D, ROWS), BF),
    ("rels", (2, EDGES), jnp.int32),
    ("ids_out", (2, 8, PICKS), jnp.int32),
    ("ids", (2, 8, PICKS), jnp.int32),
    ("gath", (256, 512), BF),
    ("table", (BLOCKS,) + BLOCK, BF),
    ("served", (2, 3) + BLOCK, BF),
    ("picked", (2, 3) + BLOCK, BF),
    ("head_vec", (D, 2 * EDGES), F32),
    ("rel_vec", (D, 2 * EDGES), F32),
    ("head_grad", (D, 2 * EDGES), BF),
    ("rel_grad", (D, 2 * EDGES), BF),
    ("pick_grad", (2, 3) + BLOCK, BF),
    ("pick_in", (2, 3) + BLOCK, BF),
    ("stage", (16,) + BLOCK, BF),
    ("sib", (16,) + BLOCK, BF),
    ("xs", (8,) + BLOCK, BF),
    ("xbuf", (8,) + BLOCK, BF),
    ("rel_cols", (2 * EDGES, 128), jnp.int32),
    ("head_cols", (2 * EDGES, 128), jnp.int32),
    ("pick_cols", (2 * PICKS, 128), jnp.int32),
    ("beside", (2,) + BLOCK, F32),
    ("within", (8,) + BLOCK, F32),
    ("acc", BLOCK, F32),
    ("zs", (7,) + BLOCK, BF),
    ("zbuf", (2, 4) + BLOCK, BF),
    ("head_sum", (8,) + BLOCK, F32),
    ("ent_stage", (4,) + BLOCK, BF),
    ("ent_sib", (4,) + BLOCK, BF),
    ("ent_sum", (4,) + BLOCK, BF),
    ("ent_far", (4,) + BLOCK, BF),
    ("ent_end", (8,) + BLOCK, BF),
    ("fin", (256, 512), BF),
    ("parts", (8, SLOT, 512), BF),
)
SEMAPHORES = (
    ("a", (8,)), ("i", (2,)), ("p", (2, 3)), ("z", (2, 2, 5)), ("x", (2, 8)), ("s", (16,)),
    ("n", (2, 3)), ("t", (16,)), ("w", (2, 8)), ("v", (2, 2, 4)),
    ("es", (4,)), ("ef", (4,)), ("ee", (4,)), ("c", (8,)), ("o", (9,)),
)


class Held:
    pass


def step_kernel(
    entity_in, entity_state, relation, heads, tails, negs, relation_ids, rel_out, ent_out, state_out, *scratch
):
    m = Held()
    names = [name for name, _, _ in BUFFERS]
    for name, _ in SEMAPHORES:
        names += [name + "_send", name + "_recv"]
    for name, ref in zip(names, scratch, strict=True):
        setattr(m, name, ref)
    at = Place()
    top, low = pl.ds(0, CUT), pl.ds(CUT, D - CUT)
    halves = (top, low)
    barrier = greet(at)
    load = pltpu.make_async_copy(entity_in, m.entity, m.o_recv.at[8])
    load.start()

    m.pad[...] = jnp.zeros_like(m.pad)
    m.pad[:OWN_REL, :D] = relation[...]
    m.shard[...] = m.pad[...].astype(BF)
    for b in range(2):
        m.ids_out[b, :, :EDGES] = jnp.broadcast_to(tails[b:b + 1, :], (8, EDGES))
        m.ids_out[b, :, EDGES:] = jnp.broadcast_to(negs[b], (8, NEG))
    ids = relation_ids[...]
    m.rels[...] = ids + (SLOT - OWN_REL) * ((ids * 36158) >> 20)
    pl.semaphore_wait(barrier, 21)

    slot = lax.rem(at.y, 2) * 4 + at.e
    here = at.c == at.y // 2
    mine = m.gath.at[pl.ds(pl.multiple_of(slot * SLOT, SLOT), SLOT), :]
    for k in range(8):
        y, xh = lax.rem(at.y + k // 2, 4), lax.rem(at.xh + k % 2, 2)
        peer = at.group(y, xh * 2 + at.y // 2)
        if k == 0:
            @pl.when(here)
            def _():
                pltpu.make_async_copy(m.shard, mine, m.a_recv.at[slot]).start()

            @pl.when(jnp.logical_not(here))
            def _():
                send(m.shard, mine, m.a_send.at[0], m.a_recv.at[slot], peer)
        else:
            send(m.shard, mine, m.a_send.at[k], m.a_recv.at[slot], peer)
    for b, peer in enumerate((at.next, at.prev)):
        send(m.ids_out.at[b], m.ids.at[b], m.i_send.at[b], m.i_recv.at[b], peer)
    load.wait()
    m.own[...] = m.entity[...].astype(BF)
    for b in range(2):
        m.rel_cols[b * EDGES:(b + 1) * EDGES, :] = columns(m.rels[b:b + 1, :])
        m.head_cols[b * EDGES:(b + 1) * EDGES, :] = columns(heads[b:b + 1, :])

    for k in range(8):
        settle(m.gath.at[pl.ds(k * SLOT, SLOT), :], m.a_recv.at[k])
    m.table[at.block(at.xl, 0, at.c)] = m.gath[...].astype(F32).T[:D].astype(BF)

    def ring_block(j, part):
        return m.table.at[at.incoming(j, at.xl, at.c), halves[part], :]

    def along_z(j, way, step, part):
        ref = ring_block(j, part)
        send(ref, ref, m.z_send.at[part, way, step], m.z_recv.at[part, way, step], at.along_z(way))

    def along_x(j, part):
        ref = ring_block(j, part)
        send(ref, ref, m.x_send.at[part, j], m.x_recv.at[part, j], (at.x_up, at.x_down)[part])

    def to_sibling(j, xl, q):
        ref = m.table.at[at.incoming(j, xl, at.c)]
        send(ref, ref, m.s_send.at[q], m.s_recv.at[q], at.sibling)

    for part in range(2):
        along_z(0, 0, 0, part)
        along_z(0, 1, 0, part)
        along_x(0, part)
    to_sibling(0, at.xl, 0)

    for b in range(2):
        settle(m.ids.at[b], m.i_recv.at[b])

    @pl.loop(0, 6)
    def _(t):
        b, n = t // 3, t % 3
        m.served[b, n] = dot(m.own[...], onehot(m.ids[b, 0:1, lanes(n)], 0, ROWS)).astype(BF)
        send(
            m.served.at[b, n], m.picked.at[b, n], m.p_send.at[b, n], m.p_recv.at[b, n],
            (lax.rem(at.d + 63 + 2 * b, 64), at.e),
        )

    for b in range(2):
        m.pick_cols[b * PICKS:(b + 1) * PICKS, :] = columns(m.ids[b, 0:1, :])
    m.rel_vec[...] = jnp.zeros_like(m.rel_vec)

    def head_rows(t):
        m.head_vec[:, lanes(t)] = dot(
            m.own[...], onehot(heads[pl.ds(t // 2, 1), lanes(t % 2)], 0, ROWS)
        )

    def absorb(k, xl, q):
        settle(m.table.at[at.incoming(k, xl, 1 - at.c)], m.s_recv.at[q])
        n, other = at.incoming(k, xl, 0), at.incoming(k, xl, 1)
        for b in range(2):
            m.rel_vec[:, b * EDGES:(b + 1) * EDGES] += dot(
                m.table[n], onehot(m.rels[b:b + 1, :], n * 256, 256)
            ) + dot(m.table[other], onehot(m.rels[b:b + 1, :], other * 256, 256))

    @pl.loop(1, 12)
    def _(j):
        way, step = at.ring_way(j), at.ring_step(j)
        split = jnp.logical_and(at.even, j == 7)
        for part in range(2):
            @pl.when(jnp.logical_and(j <= 7, jnp.logical_not(split)))
            def _():
                settle(ring_block(j, part), m.z_recv.at[part, way, step])

            @pl.when(split)
            def _():
                settle(ring_block(j, part), m.z_recv.at[part, part, 3])

            @pl.when(jnp.logical_and(j <= 6, at.ring_sent(way, step + 1, part)))
            def _():
                along_z(j, way, step + 1, part)

            @pl.when(j <= 7)
            def _():
                along_x(j, part)

        @pl.when(j <= 7)
        def _():
            to_sibling(j, at.xl, j)

        @pl.when(jnp.logical_and(j >= 2, j <= 9))
        def _():
            for part in range(2):
                settle(
                    m.table.at[at.incoming(j - 2, 1 - at.xl, at.c), halves[part], :],
                    m.x_recv.at[part, j - 2],
                )
            to_sibling(j - 2, 1 - at.xl, 6 + j)

        @pl.when(j <= 4)
        def _():
            head_rows(j - 1)

        @pl.when(jnp.logical_and(j >= 2, j <= 9))
        def _():
            absorb(j - 2, at.xl, j - 2)

        @pl.when(j >= 4)
        def _():
            absorb(j - 4, 1 - at.xl, 4 + j)

    kept = []
    for b in range(2):
        for n in range(3):
            settle(m.picked.at[b, n], m.p_recv.at[b, n])
        span = slice(b * EDGES, (b + 1) * EDGES)
        h_re, h_im = m.head_vec[:HALF, span], m.head_vec[HALF:, span]
        r_re, r_im = m.rel_vec[:HALF, span], m.rel_vec[HALF:, span]
        q = jnp.concatenate([h_re * r_re - h_im * r_im, h_re * r_im + h_im * r_re], axis=0)
        q_low = q.astype(BF)
        tail = jnp.concatenate([m.picked[b, 0], m.picked[b, 1]], axis=1).astype(F32)
        positive = jnp.sum(q * tail, axis=0, keepdims=True)
        slope = -jax.nn.sigmoid(-positive)
        scores = dot(m.picked[b, 2], q_low, ((0,), (0,)))
        neg_slope = jax.nn.sigmoid(scores).astype(BF)
        tail_grad = (slope * q).astype(BF)
        m.pick_grad[b, 0] = tail_grad[:, :256]
        m.pick_grad[b, 1] = tail_grad[:, 256:]
        m.pick_grad[b, 2] = dot(q_low, neg_slope, ACROSS).astype(BF)
        for n in range(3):
            send(
                m.pick_grad.at[b, n], m.pick_in.at[b, n], m.n_send.at[b, n], m.n_recv.at[b, n],
                (at.next, at.prev)[b],
            )
        kept.append((slope, neg_slope))

    for b in range(2):
        span = slice(b * EDGES, (b + 1) * EDGES)
        h_re, h_im = m.head_vec[:HALF, span], m.head_vec[HALF:, span]
        r_re, r_im = m.rel_vec[:HALF, span], m.rel_vec[HALF:, span]
        slope, neg_slope = kept[b]
        tail = jnp.concatenate([m.picked[b, 0], m.picked[b, 1]], axis=1).astype(F32)
        u = slope * tail + dot(m.picked[b, 2], neg_slope)
        u_re, u_im = u[:HALF], u[HALF:]
        m.rel_grad[:, span] = jnp.concatenate(
            [u_re * h_re + u_im * h_im, u_im * h_re - u_re * h_im], axis=0
        ).astype(BF)
        m.head_grad[:, span] = jnp.concatenate(
            [u_re * r_re + u_im * r_im, u_im * r_re - u_re * r_im], axis=0
        ).astype(BF)

    def rel_pair(j, xl, q):
        mine, other = at.outgoing(j, xl, at.c), at.outgoing(j, xl, 1 - at.c)
        pair = dot(m.rel_grad[...], spread(m.rel_cols[...], (mine * 256, other * 256)))
        m.stage[q] = pair[:, 256:].astype(BF)
        send(m.stage.at[q], m.sib.at[q], m.t_send.at[q], m.t_recv.at[q], at.sibling)
        return pair[:, :256]

    def to_x(k):
        settle(m.sib.at[k], m.t_recv.at[k])
        m.xs[k] = (m.beside[k % 2] + m.sib[k].astype(F32)).astype(BF)
        for side, peer in ((0, at.x_up), (1, at.x_down)):
            send(
                m.xs.at[k, halves[side], :], m.xbuf.at[k, halves[side], :],
                m.w_send.at[side, k], m.w_recv.at[side, k], peer,
            )

    def head_pair(k):
        pair = dot(m.head_grad[...], spread(m.head_cols[...], (k * 512, k * 512 + 256)))
        m.head_sum[2 * k] = pair[:, :256]
        m.head_sum[2 * k + 1] = pair[:, 256:]

    def entity_pair(k):
        total = None
        for b in range(2):
            for i in range(3):
                start = b * PICKS + i * 256
                term = dot(
                    m.pick_in[b, i],
                    spread(m.pick_cols[start:start + 256, :], (k * 512, k * 512 + 256)),
                )
                total = term if total is None else total + term
        m.head_sum[2 * k] += total[:, :256]
        m.head_sum[2 * k + 1] += total[:, 256:]

    def entity_swap(k):
        m.ent_stage[k] = m.head_sum[(1 - at.c) * 4 + k].astype(BF)
        send(m.ent_stage.at[k], m.ent_sib.at[k], m.es_send.at[k], m.es_recv.at[k], at.sibling)

    def entity_far(k):
        settle(m.ent_sib.at[k], m.es_recv.at[k])
        m.ent_sum[k] = (m.head_sum[at.c * 4 + k] + m.ent_sib[k].astype(F32)).astype(BF)
        send(m.ent_sum.at[k], m.ent_far.at[k], m.ef_send.at[k], m.ef_recv.at[k], at.far)

    def z_step(j):
        settle(m.sib.at[8 + j], m.t_recv.at[8 + j])
        for side in range(2):
            settle(m.xbuf.at[j, halves[side], :], m.w_recv.at[side, j])
        m.acc[...] = m.within[j] + m.sib[8 + j].astype(F32) + m.xbuf[j].astype(F32)
        way, step = (j + 1) % 2, (j + 1) // 2

        for part in range(2):
            rows = (slice(0, CUT), slice(CUT, D))[part]

            def add(side, last):
                settle(m.zbuf.at[side, last, halves[part], :], m.v_recv.at[part, side, last])
                m.acc[rows, :] += m.zbuf[side, last, rows, :].astype(F32)

            @pl.when(jnp.logical_or(j == part + 1, jnp.logical_and(j >= 3, j <= 6)))
            def _():
                add(way, step - 1)

            @pl.when(j == 7)
            def _():
                add(0, 3)
                add(1, 3)

            @pl.when(j <= 6)
            def _():
                m.zs[j, rows, :] = m.acc[rows, :].astype(BF)
                side = jnp.where(j == 0, part, way)
                send(
                    m.zs.at[j, halves[part], :], m.zbuf.at[side, step, halves[part], :],
                    m.v_send.at[part, side, step], m.v_recv.at[part, side, step], at.along_z(side),
                )

    @pl.loop(0, 9)
    def _(j):
        @pl.when(j < 8)
        def _():
            m.beside[j % 2] = rel_pair(j, 1 - at.xl, j)

        @pl.when(j >= 1)
        def _():
            to_x(j - 1)

    @pl.loop(0, 8)
    def _(j):
        m.within[j] = rel_pair(j, at.xl, 8 + j)

    @pl.loop(0, 8)
    def _(j):
        z_step(j)

        @pl.when(j < 4)
        def _():
            head_pair(j)

        @pl.when(j == 4)
        def _():
            for b in range(2):
                for n in range(3):
                    settle(m.pick_in.at[b, n], m.n_recv.at[b, n])

            @pl.loop(0, 2)
            def _(i):
                entity_pair((1 - at.c) * 2 + i)
                entity_swap(2 * i)
                entity_swap(2 * i + 1)

            @pl.loop(0, 2)
            def _(i):
                entity_pair(at.c * 2 + i)
                entity_far(2 * i)
                entity_far(2 * i + 1)

    m.fin[...] = jnp.concatenate([m.acc[...], jnp.zeros((512 - D, 256), F32)], axis=0).T.astype(BF)
    source = at.y * 2 + at.xh
    for k in range(8):
        y, e = 2 * at.c + k // 4, k % 4
        mine_too = jnp.logical_and(at.y == y, at.e == e)
        piece = m.fin.at[pl.ds(k * SLOT, SLOT), :]

        @pl.when(mine_too)
        def _():
            pltpu.make_async_copy(piece, m.parts.at[source], m.c_recv.at[source]).start()

        @pl.when(jnp.logical_not(mine_too))
        def _():
            send(piece, m.parts.at[source], m.c_send.at[k], m.c_recv.at[source], at.group(y, e))

    @pl.loop(0, 4)
    def _(k):
        settle(m.ent_far.at[k], m.ef_recv.at[k])
        n = at.c * 4 + k
        m.ent_end[n] = (m.ent_sum[k].astype(F32) + m.ent_far[k].astype(F32)).astype(BF)
        send(m.ent_end.at[n], m.ent_end.at[n], m.ee_send.at[k], m.ee_recv.at[k], at.sibling)

    for k in range(8):
        settle(m.parts.at[k], m.c_recv.at[k])
    rel_out[...] = jnp.sum(m.parts[...].astype(F32), axis=0)
    def adagrad(n):
        grad = m.ent_end[n].astype(F32)
        history = entity_state[:, lanes(n)] + jnp.sum(grad * grad, axis=0, keepdims=True) * (1.0 / D)
        state_out[:, lanes(n)] = history
        m.entity[:, lanes(n)] -= grad * (LEARN_RATE / jnp.sqrt(history))
        pltpu.make_async_copy(m.entity.at[:, lanes(n)], ent_out.at[:, lanes(n)], m.o_recv.at[n]).start()

    @pl.loop(0, 4)
    def _(k):
        adagrad(at.c * 4 + k)

    @pl.loop(0, 4)
    def _(k):
        settle(m.ent_end.at[(1 - at.c) * 4 + k], m.ee_recv.at[k])
        adagrad((1 - at.c) * 4 + k)

    for n in range(8):
        pltpu.make_async_copy(m.entity.at[:, lanes(n)], ent_out.at[:, lanes(n)], m.o_recv.at[n]).wait()

    @pl.when(jnp.logical_not(here))
    def _():
        settle(m.shard, m.a_send.at[0])

    for k in range(1, 8):
        settle(m.shard, m.a_send.at[k])
    for k in range(8):
        y, e = 2 * at.c + k // 4, k % 4

        @pl.when(jnp.logical_not(jnp.logical_and(at.y == y, at.e == e)))
        def _():
            settle(m.parts.at[0], m.c_send.at[k])

    one = m.stage.at[0]
    for b in range(2):
        settle(m.ids_out.at[b], m.i_send.at[b])
        for n in range(3):
            settle(one, m.p_send.at[b, n])
            settle(one, m.n_send.at[b, n])
        half = m.stage.at[0, halves[b], :]
        for way in range(2):
            for step in range(5):
                @pl.when(at.ring_sent(way, step, b))
                def _():
                    settle(half, m.z_send.at[b, way, step])

            for step in range(3):
                settle(half, m.v_send.at[b, way, step + 1])
        settle(half, m.v_send.at[b, b, 0])
        for j in range(8):
            settle(half, m.x_send.at[b, j])
            settle(half, m.w_send.at[b, j])
    for q in range(16):
        settle(one, m.s_send.at[q])
        settle(one, m.t_send.at[q])
    for k in range(4):
        settle(one, m.es_send.at[k])
        settle(one, m.ef_send.at[k])
        settle(one, m.ee_send.at[k])


def whole_step(entity, entity_state, relation, heads, tails, negs, relation_ids):
    vmem = pl.BlockSpec(memory_space=pltpu.VMEM)
    anywhere = pl.BlockSpec(memory_space=pl.ANY)
    scratch = [pltpu.VMEM(shape, kind) for _, shape, kind in BUFFERS]
    for _, shape in SEMAPHORES:
        scratch += [DMA(shape), DMA(shape)]
    return pl.pallas_call(
        step_kernel,
        out_shape=(
            jax.ShapeDtypeStruct((SLOT, 512), F32),
            jax.ShapeDtypeStruct((D, ROWS), F32),
            jax.ShapeDtypeStruct((1, ROWS), F32),
        ),
        in_specs=[anywhere] + [vmem] * 6,
        out_specs=(vmem, anywhere, vmem),
        scratch_shapes=scratch,
        compiler_params=pltpu.CompilerParams(
            collective_id=0, has_side_effects=True, vmem_limit_bytes=60 * MIB
        ),
        name="whole_step",
    )(entity, entity_state, relation, heads, tails, negs, relation_ids)


def local(
    entity_emb,
    entity_state,
    relation_emb,
    relation_state,
    head_rows,
    tail_rows,
    relation_ids,
    negative_rows,
):
    relation_grad, new_entity, new_entity_state = whole_step(
        entity_emb.T, entity_state[None], relation_emb, head_rows, tail_rows, negative_rows, relation_ids
    )
    relation_grad = relation_grad[:OWN_REL, :D]
    new_relation_state = relation_state + jnp.mean(relation_grad * relation_grad, axis=-1)
    new_relation_emb = relation_emb - LEARN_RATE * relation_grad / jnp.sqrt(new_relation_state)[:, None]
    return (new_entity.T, new_entity_state[0], new_relation_emb, new_relation_state)


def solution(mesh):
    placed = (
        P("dom", None),
        P("dom"),
        P(("dom", "edge"), None),
        P(("dom", "edge")),
        P(None, ("dom", "edge")),
        P(None, ("dom", "edge")),
        P(None, ("dom", "edge")),
        P(None, ("dom", "edge"), None),
    )
    return jax.shard_map(
        local,
        mesh=mesh,
        in_specs=placed,
        out_specs=(P("dom", None), P("dom"), P(("dom", "edge"), None), P(("dom", "edge"))),
        check_vma=False,
    )
```

```python
import jax
import jax.numpy as jnp
from jax import lax
from jax.experimental import pallas as pl
from jax.experimental.pallas import tpu as pltpu
from jax.sharding import PartitionSpec as P

LEARN_RATE = 0.5
D = 400
HALF = 200
ROWS = 2048
EDGES = 512
NEG = 256
PICKS = EDGES + NEG
OWN_REL = 29
SLOT = 32
CUT = 208
Z = 8
BLOCKS = 32
MIB = 1 << 20
MESH = pl.DeviceIdType.MESH
BF = jnp.bfloat16
F32 = jnp.float32
ACROSS = ((1,), (1,))


class Place:
    def __init__(self):
        self.d = lax.axis_index("dom")
        self.e = lax.axis_index("edge")
        self.y = lax.rem(self.d, 4)
        self.z = lax.rem(self.d // 4, Z)
        self.xl = self.d // 32
        self.even = jnp.logical_and(self.y > 0, self.y < 3)
        self.xh = self.e // 2
        self.c = lax.rem(self.e, 2)
        x = self.xh * 2 + self.xl
        other = lax.rem(self.d + 32, 64)
        self.x_up = (other, (lax.rem(x + 1, 4) // 2) * 2 + self.c)
        self.x_down = (other, (lax.rem(x + 3, 4) // 2) * 2 + self.c)
        self.z_up = self.along_z(0)
        self.z_down = self.along_z(1)
        self.next = (lax.rem(self.d + 1, 64), self.e)
        self.prev = (lax.rem(self.d + 63, 64), self.e)
        self.sibling = (self.d, self.xh * 2 + 1 - self.c)
        self.far = (self.d, (1 - self.xh) * 2 + self.c)

    def along_z(self, way):
        return (self.xl * 32 + lax.rem(self.z + 1 + 6 * way, Z) * 4 + self.y, self.e)

    def group(self, y, e):
        return (self.d - self.y + y, e)

    def block(self, xl, offset, half):
        return (xl * Z + lax.rem(self.z + offset + Z, Z)) * 2 + half

    def ring_step(self, j):
        return (jnp.where(self.even, 0x32211000, 0x43121000) >> (4 * jnp.minimum(j, 7))) & 15

    def ring_way(self, j):
        return (jnp.where(self.even, 0x54, jnp.where(self.y == 0, 0x24, 0xDA)) >> j) & 1

    def ring_sent(self, way, step, part):
        most = jnp.where(self.even, jnp.where(part == way, 4, 3), jnp.where(way == self.y // 3, 5, 2))
        return step < most

    def incoming(self, j, xl, half):
        away = self.ring_step(j) + 1
        away = jnp.where(self.ring_way(j) == 1, away, -away)
        return self.block(xl, jnp.where(j == 0, 0, away), half)

    def outgoing(self, j, xl, half):
        away = 4 - (j + 1) // 2
        return self.block(xl, jnp.where(j % 2 == 1, away, -away), half)


def greet(at):
    barrier = pltpu.get_barrier_semaphore()
    where = at.y * 4 + at.e
    for k in range(1, 16):
        peer = lax.rem(where + k, 16)
        pl.semaphore_signal(
            barrier, inc=1, device_id=at.group(peer // 4, lax.rem(peer, 4)), device_id_type=MESH
        )
    for peer in (at.x_up, at.x_down, at.z_up, at.z_down, at.next, at.prev):
        pl.semaphore_signal(barrier, inc=1, device_id=peer, device_id_type=MESH)
    return barrier


def send(src, dst, send_sem, recv_sem, peer):
    pltpu.make_async_remote_copy(
        src_ref=src,
        dst_ref=dst,
        send_sem=send_sem,
        recv_sem=recv_sem,
        device_id=peer,
        device_id_type=MESH,
    ).start()


def settle(ref, sem):
    pltpu.make_async_copy(ref, ref, sem).wait()


def onehot(ids, base, rows):
    at = lax.broadcasted_iota(jnp.int32, (rows, ids.shape[1]), 0) + base
    return jnp.where(at == ids, 1.0, 0.0).astype(BF)


def columns(ids):
    return jnp.broadcast_to(ids, (128, ids.shape[1])).T


def spread(cols, bases):
    lane = lax.broadcasted_iota(jnp.int32, cols.shape, 1)
    tiles = []
    for base in bases:
        for k in (0, 128):
            tiles.append(jnp.where(cols - (base + k) == lane, 1.0, 0.0).astype(BF))
    return jnp.concatenate(tiles, axis=1)


def dot(a, b, over=((1,), (0,))):
    return lax.dot_general(a, b, (over, ((), ())), preferred_element_type=F32)


def lanes(k):
    return pl.ds(pl.multiple_of(k * 256, 256), 256)


BLOCK = (D, 256)
DMA = pltpu.SemaphoreType.DMA
BUFFERS = (
    ("entity", (D, ROWS), F32),
    ("pad", (SLOT, 512), F32),
    ("shard", (SLOT, 512), BF),
    ("own", (D, ROWS), BF),
    ("rels", (2, EDGES), jnp.int32),
    ("ids_out", (2, 8, PICKS), jnp.int32),
    ("ids", (2, 8, PICKS), jnp.int32),
    ("gath", (256, 512), BF),
    ("table", (BLOCKS,) + BLOCK, BF),
    ("served", (2, 3) + BLOCK, BF),
    ("picked", (2, 3) + BLOCK, BF),
    ("head_vec", (D, 2 * EDGES), F32),
    ("rel_vec", (D, 2 * EDGES), F32),
    ("head_grad", (D, 2 * EDGES), BF),
    ("rel_grad", (D, 2 * EDGES), BF),
    ("pick_grad", (2, 3) + BLOCK, BF),
    ("pick_in", (2, 3) + BLOCK, BF),
    ("stage", (16,) + BLOCK, BF),
    ("sib", (16,) + BLOCK, BF),
    ("xs", (8,) + BLOCK, BF),
    ("xbuf", (8,) + BLOCK, BF),
    ("rel_cols", (2 * EDGES, 128), jnp.int32),
    ("head_cols", (2 * EDGES, 128), jnp.int32),
    ("pick_cols", (2 * PICKS, 128), jnp.int32),
    ("beside", (2,) + BLOCK, F32),
    ("within", (8,) + BLOCK, F32),
    ("acc", BLOCK, F32),
    ("zs", (7,) + BLOCK, BF),
    ("zbuf", (2, 4) + BLOCK, BF),
    ("head_sum", (8,) + BLOCK, F32),
    ("ent_stage", (4,) + BLOCK, BF),
    ("ent_sib", (4,) + BLOCK, BF),
    ("ent_sum", (4,) + BLOCK, BF),
    ("ent_far", (4,) + BLOCK, BF),
    ("ent_end", (8,) + BLOCK, BF),
    ("fin", (256, 512), BF),
    ("parts", (8, SLOT, 512), BF),
)
SEMAPHORES = (
    ("a", (8,)), ("i", (2,)), ("p", (2, 3)), ("z", (2, 2, 5)), ("x", (2, 8)), ("s", (16,)),
    ("n", (2, 3)), ("t", (16,)), ("w", (2, 8)), ("v", (2, 2, 4)),
    ("es", (4,)), ("ef", (4,)), ("ee", (4,)), ("c", (8,)), ("o", (9,)),
)


class Held:
    pass


def step_kernel(
    entity_in, entity_state, relation, heads, tails, negs, relation_ids, rel_out, ent_out, state_out, *scratch
):
    m = Held()
    names = [name for name, _, _ in BUFFERS]
    for name, _ in SEMAPHORES:
        names += [name + "_send", name + "_recv"]
    for name, ref in zip(names, scratch, strict=True):
        setattr(m, name, ref)
    at = Place()
    top, low = pl.ds(0, CUT), pl.ds(CUT, D - CUT)
    halves = (top, low)
    barrier = greet(at)
    load = pltpu.make_async_copy(entity_in, m.entity, m.o_recv.at[8])
    load.start()

    m.pad[...] = jnp.zeros_like(m.pad)
    m.pad[:OWN_REL, :D] = relation[...]
    m.shard[...] = m.pad[...].astype(BF)
    for b in range(2):
        m.ids_out[b, :, :EDGES] = jnp.broadcast_to(tails[b:b + 1, :], (8, EDGES))
        m.ids_out[b, :, EDGES:] = jnp.broadcast_to(negs[b], (8, NEG))
    ids = relation_ids[...]
    m.rels[...] = ids + (SLOT - OWN_REL) * ((ids * 36158) >> 20)
    pl.semaphore_wait(barrier, 21)

    slot = lax.rem(at.y, 2) * 4 + at.e
    here = at.c == at.y // 2
    mine = m.gath.at[pl.ds(pl.multiple_of(slot * SLOT, SLOT), SLOT), :]
    for k in range(8):
        y, xh = lax.rem(at.y + k // 2, 4), lax.rem(at.xh + k % 2, 2)
        peer = at.group(y, xh * 2 + at.y // 2)
        if k == 0:
            @pl.when(here)
            def _():
                pltpu.make_async_copy(m.shard, mine, m.a_recv.at[slot]).start()

            @pl.when(jnp.logical_not(here))
            def _():
                send(m.shard, mine, m.a_send.at[0], m.a_recv.at[slot], peer)
        else:
            send(m.shard, mine, m.a_send.at[k], m.a_recv.at[slot], peer)
    for b, peer in enumerate((at.next, at.prev)):
        send(m.ids_out.at[b], m.ids.at[b], m.i_send.at[b], m.i_recv.at[b], peer)
    load.wait()
    m.own[...] = m.entity[...].astype(BF)
    for b in range(2):
        m.rel_cols[b * EDGES:(b + 1) * EDGES, :] = columns(m.rels[b:b + 1, :])
        m.head_cols[b * EDGES:(b + 1) * EDGES, :] = columns(heads[b:b + 1, :])

    for k in range(8):
        settle(m.gath.at[pl.ds(k * SLOT, SLOT), :], m.a_recv.at[k])
    m.table[at.block(at.xl, 0, at.c)] = m.gath[...].astype(F32).T[:D].astype(BF)

    def ring_block(j, part):
        return m.table.at[at.incoming(j, at.xl, at.c), halves[part], :]

    def along_z(j, way, step, part):
        ref = ring_block(j, part)
        send(ref, ref, m.z_send.at[part, way, step], m.z_recv.at[part, way, step], at.along_z(way))

    def along_x(j, part):
        ref = ring_block(j, part)
        send(ref, ref, m.x_send.at[part, j], m.x_recv.at[part, j], (at.x_up, at.x_down)[part])

    def to_sibling(j, xl, q):
        ref = m.table.at[at.incoming(j, xl, at.c)]
        send(ref, ref, m.s_send.at[q], m.s_recv.at[q], at.sibling)

    for part in range(2):
        along_z(0, 0, 0, part)
        along_z(0, 1, 0, part)
        along_x(0, part)
    to_sibling(0, at.xl, 0)

    for b in range(2):
        settle(m.ids.at[b], m.i_recv.at[b])

    @pl.loop(0, 6)
    def _(t):
        b, n = t // 3, t % 3
        m.served[b, n] = dot(m.own[...], onehot(m.ids[b, 0:1, lanes(n)], 0, ROWS)).astype(BF)
        send(
            m.served.at[b, n], m.picked.at[b, n], m.p_send.at[b, n], m.p_recv.at[b, n],
            (lax.rem(at.d + 63 + 2 * b, 64), at.e),
        )

    for b in range(2):
        m.pick_cols[b * PICKS:(b + 1) * PICKS, :] = columns(m.ids[b, 0:1, :])
    m.rel_vec[...] = jnp.zeros_like(m.rel_vec)

    def head_rows(t):
        m.head_vec[:, lanes(t)] = dot(
            m.own[...], onehot(heads[pl.ds(t // 2, 1), lanes(t % 2)], 0, ROWS)
        )

    def absorb(k, xl, q):
        settle(m.table.at[at.incoming(k, xl, 1 - at.c)], m.s_recv.at[q])
        n, other = at.incoming(k, xl, 0), at.incoming(k, xl, 1)
        for b in range(2):
            m.rel_vec[:, b * EDGES:(b + 1) * EDGES] += dot(
                m.table[n], onehot(m.rels[b:b + 1, :], n * 256, 256)
            ) + dot(m.table[other], onehot(m.rels[b:b + 1, :], other * 256, 256))

    @pl.loop(1, 12)
    def _(j):
        way, step = at.ring_way(j), at.ring_step(j)
        split = jnp.logical_and(at.even, j == 7)
        for part in range(2):
            @pl.when(jnp.logical_and(j <= 7, jnp.logical_not(split)))
            def _():
                settle(ring_block(j, part), m.z_recv.at[part, way, step])

            @pl.when(split)
            def _():
                settle(ring_block(j, part), m.z_recv.at[part, part, 3])

            @pl.when(jnp.logical_and(j <= 6, at.ring_sent(way, step + 1, part)))
            def _():
                along_z(j, way, step + 1, part)

            @pl.when(j <= 7)
            def _():
                along_x(j, part)

        @pl.when(j <= 7)
        def _():
            to_sibling(j, at.xl, j)

        @pl.when(jnp.logical_and(j >= 2, j <= 9))
        def _():
            for part in range(2):
                settle(
                    m.table.at[at.incoming(j - 2, 1 - at.xl, at.c), halves[part], :],
                    m.x_recv.at[part, j - 2],
                )
            to_sibling(j - 2, 1 - at.xl, 6 + j)

        @pl.when(j <= 4)
        def _():
            head_rows(j - 1)

        @pl.when(jnp.logical_and(j >= 2, j <= 9))
        def _():
            absorb(j - 2, at.xl, j - 2)

        @pl.when(j >= 4)
        def _():
            absorb(j - 4, 1 - at.xl, 4 + j)

    kept = []
    for b in range(2):
        for n in range(3):
            settle(m.picked.at[b, n], m.p_recv.at[b, n])
        span = slice(b * EDGES, (b + 1) * EDGES)
        h_re, h_im = m.head_vec[:HALF, span], m.head_vec[HALF:, span]
        r_re, r_im = m.rel_vec[:HALF, span], m.rel_vec[HALF:, span]
        q = jnp.concatenate([h_re * r_re - h_im * r_im, h_re * r_im + h_im * r_re], axis=0)
        q_low = q.astype(BF)
        tail = jnp.concatenate([m.picked[b, 0], m.picked[b, 1]], axis=1).astype(F32)
        positive = jnp.sum(q * tail, axis=0, keepdims=True)
        slope = -jax.nn.sigmoid(-positive)
        scores = dot(m.picked[b, 2], q_low, ((0,), (0,)))
        neg_slope = jax.nn.sigmoid(scores).astype(BF)
        tail_grad = (slope * q).astype(BF)
        m.pick_grad[b, 0] = tail_grad[:, :256]
        m.pick_grad[b, 1] = tail_grad[:, 256:]
        m.pick_grad[b, 2] = dot(q_low, neg_slope, ACROSS).astype(BF)
        for n in range(3):
            send(
                m.pick_grad.at[b, n], m.pick_in.at[b, n], m.n_send.at[b, n], m.n_recv.at[b, n],
                (at.next, at.prev)[b],
            )
        kept.append((slope, neg_slope))

    for b in range(2):
        span = slice(b * EDGES, (b + 1) * EDGES)
        h_re, h_im = m.head_vec[:HALF, span], m.head_vec[HALF:, span]
        r_re, r_im = m.rel_vec[:HALF, span], m.rel_vec[HALF:, span]
        slope, neg_slope = kept[b]
        tail = jnp.concatenate([m.picked[b, 0], m.picked[b, 1]], axis=1).astype(F32)
        u = slope * tail + dot(m.picked[b, 2], neg_slope)
        u_re, u_im = u[:HALF], u[HALF:]
        m.rel_grad[:, span] = jnp.concatenate(
            [u_re * h_re + u_im * h_im, u_im * h_re - u_re * h_im], axis=0
        ).astype(BF)
        m.head_grad[:, span] = jnp.concatenate(
            [u_re * r_re + u_im * r_im, u_im * r_re - u_re * r_im], axis=0
        ).astype(BF)

    def rel_pair(j, xl, q):
        mine, other = at.outgoing(j, xl, at.c), at.outgoing(j, xl, 1 - at.c)
        pair = dot(m.rel_grad[...], spread(m.rel_cols[...], (mine * 256, other * 256)))
        m.stage[q] = pair[:, 256:].astype(BF)
        send(m.stage.at[q], m.sib.at[q], m.t_send.at[q], m.t_recv.at[q], at.sibling)
        return pair[:, :256]

    def to_x(k):
        settle(m.sib.at[k], m.t_recv.at[k])
        m.xs[k] = (m.beside[k % 2] + m.sib[k].astype(F32)).astype(BF)
        for side, peer in ((0, at.x_up), (1, at.x_down)):
            send(
                m.xs.at[k, halves[side], :], m.xbuf.at[k, halves[side], :],
                m.w_send.at[side, k], m.w_recv.at[side, k], peer,
            )

    def head_pair(k):
        pair = dot(m.head_grad[...], spread(m.head_cols[...], (k * 512, k * 512 + 256)))
        m.head_sum[2 * k] = pair[:, :256]
        m.head_sum[2 * k + 1] = pair[:, 256:]

    def entity_pair(k):
        total = None
        for b in range(2):
            for i in range(3):
                start = b * PICKS + i * 256
                term = dot(
                    m.pick_in[b, i],
                    spread(m.pick_cols[start:start + 256, :], (k * 512, k * 512 + 256)),
                )
                total = term if total is None else total + term
        m.head_sum[2 * k] += total[:, :256]
        m.head_sum[2 * k + 1] += total[:, 256:]

    def entity_swap(k):
        m.ent_stage[k] = m.head_sum[(1 - at.c) * 4 + k].astype(BF)
        send(m.ent_stage.at[k], m.ent_sib.at[k], m.es_send.at[k], m.es_recv.at[k], at.sibling)

    def entity_far(k):
        settle(m.ent_sib.at[k], m.es_recv.at[k])
        m.ent_sum[k] = (m.head_sum[at.c * 4 + k] + m.ent_sib[k].astype(F32)).astype(BF)
        send(m.ent_sum.at[k], m.ent_far.at[k], m.ef_send.at[k], m.ef_recv.at[k], at.far)

    def z_step(j):
        settle(m.sib.at[8 + j], m.t_recv.at[8 + j])
        for side in range(2):
            settle(m.xbuf.at[j, halves[side], :], m.w_recv.at[side, j])
        m.acc[...] = m.within[j] + m.sib[8 + j].astype(F32) + m.xbuf[j].astype(F32)
        way, step = (j + 1) % 2, (j + 1) // 2

        for part in range(2):
            rows = (slice(0, CUT), slice(CUT, D))[part]

            def add(side, last):
                settle(m.zbuf.at[side, last, halves[part], :], m.v_recv.at[part, side, last])
                m.acc[rows, :] += m.zbuf[side, last, rows, :].astype(F32)

            @pl.when(jnp.logical_or(j == part + 1, jnp.logical_and(j >= 3, j <= 6)))
            def _():
                add(way, step - 1)

            @pl.when(j == 7)
            def _():
                add(0, 3)
                add(1, 3)

            @pl.when(j <= 6)
            def _():
                m.zs[j, rows, :] = m.acc[rows, :].astype(BF)
                side = jnp.where(j == 0, part, way)
                send(
                    m.zs.at[j, halves[part], :], m.zbuf.at[side, step, halves[part], :],
                    m.v_send.at[part, side, step], m.v_recv.at[part, side, step], at.along_z(side),
                )

    @pl.loop(0, 9)
    def _(j):
        @pl.when(j < 8)
        def _():
            m.beside[j % 2] = rel_pair(j, 1 - at.xl, j)

        @pl.when(j >= 1)
        def _():
            to_x(j - 1)

    @pl.loop(0, 8)
    def _(j):
        m.within[j] = rel_pair(j, at.xl, 8 + j)

        @pl.when(j < 4)
        def _():
            head_pair(j)

    @pl.loop(0, 8)
    def _(j):
        z_step(j)

        @pl.when(j == 2)
        def _():
            for b in range(2):
                for n in range(3):
                    settle(m.pick_in.at[b, n], m.n_recv.at[b, n])

            @pl.loop(0, 2)
            def _(i):
                entity_pair((1 - at.c) * 2 + i)
                entity_swap(2 * i)
                entity_swap(2 * i + 1)

            @pl.loop(0, 2)
            def _(i):
                entity_pair(at.c * 2 + i)
                entity_far(2 * i)
                entity_far(2 * i + 1)

    m.fin[...] = jnp.concatenate([m.acc[...], jnp.zeros((512 - D, 256), F32)], axis=0).T.astype(BF)
    source = at.y * 2 + at.xh
    for k in range(8):
        y, e = 2 * at.c + k // 4, k % 4
        mine_too = jnp.logical_and(at.y == y, at.e == e)
        piece = m.fin.at[pl.ds(k * SLOT, SLOT), :]

        @pl.when(mine_too)
        def _():
            pltpu.make_async_copy(piece, m.parts.at[source], m.c_recv.at[source]).start()

        @pl.when(jnp.logical_not(mine_too))
        def _():
            send(piece, m.parts.at[source], m.c_send.at[k], m.c_recv.at[source], at.group(y, e))

    @pl.loop(0, 4)
    def _(k):
        settle(m.ent_far.at[k], m.ef_recv.at[k])
        n = at.c * 4 + k
        m.ent_end[n] = (m.ent_sum[k].astype(F32) + m.ent_far[k].astype(F32)).astype(BF)
        send(m.ent_end.at[n], m.ent_end.at[n], m.ee_send.at[k], m.ee_recv.at[k], at.sibling)

    for k in range(8):
        settle(m.parts.at[k], m.c_recv.at[k])
    rel_out[...] = jnp.sum(m.parts[...].astype(F32), axis=0)
    def adagrad(n):
        grad = m.ent_end[n].astype(F32)
        history = entity_state[:, lanes(n)] + jnp.sum(grad * grad, axis=0, keepdims=True) * (1.0 / D)
        state_out[:, lanes(n)] = history
        m.entity[:, lanes(n)] -= grad * (LEARN_RATE / jnp.sqrt(history))
        pltpu.make_async_copy(m.entity.at[:, lanes(n)], ent_out.at[:, lanes(n)], m.o_recv.at[n]).start()

    @pl.loop(0, 4)
    def _(k):
        adagrad(at.c * 4 + k)

    @pl.loop(0, 4)
    def _(k):
        settle(m.ent_end.at[(1 - at.c) * 4 + k], m.ee_recv.at[k])
        adagrad((1 - at.c) * 4 + k)

    for n in range(8):
        pltpu.make_async_copy(m.entity.at[:, lanes(n)], ent_out.at[:, lanes(n)], m.o_recv.at[n]).wait()

    @pl.when(jnp.logical_not(here))
    def _():
        settle(m.shard, m.a_send.at[0])

    for k in range(1, 8):
        settle(m.shard, m.a_send.at[k])
    for k in range(8):
        y, e = 2 * at.c + k // 4, k % 4

        @pl.when(jnp.logical_not(jnp.logical_and(at.y == y, at.e == e)))
        def _():
            settle(m.parts.at[0], m.c_send.at[k])

    one = m.stage.at[0]
    for b in range(2):
        settle(m.ids_out.at[b], m.i_send.at[b])
        for n in range(3):
            settle(one, m.p_send.at[b, n])
            settle(one, m.n_send.at[b, n])
        half = m.stage.at[0, halves[b], :]
        for way in range(2):
            for step in range(5):
                @pl.when(at.ring_sent(way, step, b))
                def _():
                    settle(half, m.z_send.at[b, way, step])

            for step in range(3):
                settle(half, m.v_send.at[b, way, step + 1])
        settle(half, m.v_send.at[b, b, 0])
        for j in range(8):
            settle(half, m.x_send.at[b, j])
            settle(half, m.w_send.at[b, j])
    for q in range(16):
        settle(one, m.s_send.at[q])
        settle(one, m.t_send.at[q])
    for k in range(4):
        settle(one, m.es_send.at[k])
        settle(one, m.ef_send.at[k])
        settle(one, m.ee_send.at[k])


def whole_step(entity, entity_state, relation, heads, tails, negs, relation_ids):
    vmem = pl.BlockSpec(memory_space=pltpu.VMEM)
    anywhere = pl.BlockSpec(memory_space=pl.ANY)
    scratch = [pltpu.VMEM(shape, kind) for _, shape, kind in BUFFERS]
    for _, shape in SEMAPHORES:
        scratch += [DMA(shape), DMA(shape)]
    return pl.pallas_call(
        step_kernel,
        out_shape=(
            jax.ShapeDtypeStruct((SLOT, 512), F32),
            jax.ShapeDtypeStruct((D, ROWS), F32),
            jax.ShapeDtypeStruct((1, ROWS), F32),
        ),
        in_specs=[anywhere] + [vmem] * 6,
        out_specs=(vmem, anywhere, vmem),
        scratch_shapes=scratch,
        compiler_params=pltpu.CompilerParams(
            collective_id=0, has_side_effects=True, vmem_limit_bytes=60 * MIB
        ),
        name="whole_step",
    )(entity, entity_state, relation, heads, tails, negs, relation_ids)


def local(
    entity_emb,
    entity_state,
    relation_emb,
    relation_state,
    head_rows,
    tail_rows,
    relation_ids,
    negative_rows,
):
    relation_grad, new_entity, new_entity_state = whole_step(
        entity_emb.T, entity_state[None], relation_emb, head_rows, tail_rows, negative_rows, relation_ids
    )
    relation_grad = relation_grad[:OWN_REL, :D]
    new_relation_state = relation_state + jnp.mean(relation_grad * relation_grad, axis=-1)
    new_relation_emb = relation_emb - LEARN_RATE * relation_grad / jnp.sqrt(new_relation_state)[:, None]
    return (new_entity.T, new_entity_state[0], new_relation_emb, new_relation_state)


def solution(mesh):
    placed = (
        P("dom", None),
        P("dom"),
        P(("dom", "edge"), None),
        P(("dom", "edge")),
        P(None, ("dom", "edge")),
        P(None, ("dom", "edge")),
        P(None, ("dom", "edge")),
        P(None, ("dom", "edge"), None),
    )
    return jax.shard_map(
        local,
        mesh=mesh,
        in_specs=placed,
        out_specs=(P("dom", None), P("dom"), P(("dom", "edge"), None), P(("dom", "edge"))),
        check_vma=False,
    )
```
